256 devices in a mesh: rows: 32 (over y, z), own: 8 (over x, core).
Axes of the slice: x: 4, y: 4, z: 8, core: 2. Of those that a mesh axis runs over, the one named last changes fastest.
Arguments:
- embedding: bfloat16 [1048576, 128], P(('rows', 'own')), may hold values from -6 to 6
- assignment: int32 [1048576, 1], P(('rows', 'own')), may hold values from 0 to 1023; in each aligned block of 4096 rows (0 to 4095, 4096 to 8191, ...) at most 8 rows name the same one
- sub_logit: float32 [512], P('own'), may hold values from -1 to 1
- merge_offset: int32 [512], P(('own', 'rows')), may hold values from 1 to 7
Outputs:
- sub_prob: float32 [1048576], P(('rows', 'own'))
- split_score: float32 [512], P(('own', 'rows'))
- merge_score: float32 [512], P(('own', 'rows'))
The draws below stay inside these ranges and needn't reach their ends.
Inputs may be any that keep to these rules, and one draw needn't show every extreme that they name: `assignment`: within the 4096 rows of one device (aligned blocks) no id is named by more than 8 rows, a bound that some block reaches; every id is named somewhere.
All inputs are finite; a program needn't handle non-finite values.
Results may differ from the reference program's by a relative error of at most 0.0003.
Values may be sent and summed in bfloat16 or wider, within the bound.
No kernel may reach another device: no remote copies, remote signals or barrier semaphores. Data moves between devices by JAX's collectives and lax.ppermute only.
A program may use at most 64 MiB of HBM per device.

```python
import math
import jax
import jax.numpy as jnp
import numpy as np
from jax import lax

D = 128
K_OWN = 64
ROW_DEV = 4096
CLUSTERS = 512
CAP = 8
ROWS_ALL = 1048576
N_OWN = 8


def touch_ends(entries, rng, smallest, top_value):
    longest = entries.shape.index(max(entries.shape))
    spots = []
    for shift in (0, 1):
        where = [jax.random.randint(jax.random.fold_in(rng, axis), (), 0, length) for axis, length in enumerate(entries.shape)]
        where[longest] = (where[longest] + shift) % entries.shape[longest]
        spots.append(tuple(where))
    return entries.at[spots[0]].set(smallest).at[spots[1]].set(top_value)


def block_levels(stream_key, dims, pieces, low, largest):
    factor_of = 1.0
    for dim, parts in pieces:
        draws = jax.random.uniform(jax.random.fold_in(jax.random.fold_in(stream_key, 6), dim), (parts,), jnp.float32, low / len(pieces), largest / len(pieces))
        factor_of = factor_of * jnp.repeat(jnp.exp(draws), dims[dim] // parts).reshape((-1,) + (1,) * (len(dims) - 1 - dim))
    return factor_of


def shared_out(rng, own, number, rows, amount, top, limit, lean):
    sequence = jax.random.permutation(rng, amount)
    crowded, ordinary = load_shares(amount, rows * top, limit, lean, True), load_shares(amount, rows * top, limit, lean, False)
    places = jnp.arange(amount)

    def named(tallies, rotation):
        used = int((tallies > 0).sum())
        fixed = max(1, used // 4)
        passed = fixed + (places - fixed + rotation * (used - fixed)) % max(1, amount - fixed)
        return jnp.zeros((amount,), jnp.int32).at[sequence[jnp.where(places < fixed, places, passed)]].set(jnp.asarray(tallies, jnp.int32))

    tallies = jnp.where(number % 4 == 0, named(crowded, number // 4), named(ordinary, number - number // 4 - 1))
    mixed = jax.random.permutation(jax.random.fold_in(own, 3), amount)
    giver, taker = mixed[0:amount // 2 * 2:2], mixed[1:amount // 2 * 2:2]
    room = jnp.minimum(tallies[giver] - 1, limit - tallies[taker]) // 2
    room = jnp.where((giver == sequence[0]) | (taker == sequence[0]) | (tallies[taker] == 0), 0, jnp.maximum(room, 0))
    passed = jax.random.randint(jax.random.fold_in(own, 4), (amount // 2,), 0, 1 << 20) % (room + 1)
    tallies = tallies.at[giver].add(-passed).at[taker].add(passed)
    members = jnp.searchsorted(jnp.cumsum(tallies), jnp.arange(rows * top), side="right").astype(jnp.int32)
    table = members.reshape(top, rows).T
    table = table[jax.random.permutation(jax.random.fold_in(own, 1), rows)]
    rotation = jax.random.randint(jax.random.fold_in(own, 2), (rows, 1), 0, top)
    return jnp.take_along_axis(table, (jnp.arange(top)[None, :] + rotation) % top, axis=1)


def load_shares(amount, total, limit, skew, full):
    weights = [(1 << 20) // math.isqrt(grade ** skew) + 1 for grade in range(1, amount + 1)]
    largest = limit if full else min(limit, max(-(-total // amount), total * weights[0] // sum(weights)))
    least = 1 if total - largest >= amount - 1 else 0
    given, spare = [largest] + [least] * (amount - 1), total - largest - least * (amount - 1)
    while spare > 0:
        candidates = [i for i in range(1, amount) if given[i] < largest] or [i for i in range(1, amount) if given[i] < limit]
        pool, budget = sum([weights[i] for i in candidates]), spare
        for i in candidates:
            more = min(limit - given[i], max(1, budget * weights[i] // pool), spare)
            given[i] = given[i] + more
            spare = spare - more
    return np.array(given)


def noise(key, dims, scale, bound, shards=(), held_as=jnp.bfloat16):
    factor_of = block_levels(key, dims, shards, -0.22, 0.18) if shards else 1.0
    values = jax.random.normal(key, dims, jnp.float32) * scale * factor_of
    return jnp.minimum(jnp.maximum(values, -bound), bound).astype(held_as)


def setup_inputs(seed: int = 0) -> dict:
    arg_keys = jax.random.split(jax.random.key(seed), 5)
    embedding = noise(arg_keys[0], (ROWS_ALL, D), 1.0, 6.0, ((0, 256),))
    assignment_keys = jax.random.split(jax.random.fold_in(arg_keys[1], 1), ROWS_ALL // ROW_DEV)
    assignment_turns = jax.random.permutation(jax.random.fold_in(arg_keys[1], 3), ROWS_ALL // ROW_DEV)
    assignment = jax.vmap(lambda own, number: shared_out(jax.random.fold_in(arg_keys[1], 2), own, number, ROW_DEV, 2 * CLUSTERS, 1, CAP, 2))(assignment_keys, assignment_turns).reshape((ROWS_ALL, 1))
    sub_logit = jnp.clip(jax.random.uniform(arg_keys[2], (CLUSTERS,), jnp.float32, -1.0, 1.0) * block_levels(arg_keys[2], (CLUSTERS,), ((0, 8),), -0.4, 0.0), -1.0, 1.0)
    merge_offset = touch_ends(jax.random.randint(arg_keys[3], (CLUSTERS,), 1, N_OWN), jax.random.fold_in(arg_keys[3], 1), 1, N_OWN - 1).astype(jnp.int32)
    return {"embedding": embedding, "assignment": assignment, "sub_logit": sub_logit, "merge_offset": merge_offset}


HIGH = lax.Precision.HIGHEST

def slot_table(expert):
    ordering = jnp.argsort(expert, stable=True)
    ranked = expert[ordering]
    leading = jnp.searchsorted(ranked, ranked, side='left').astype(jnp.int32)
    position = jnp.arange(expert.shape[0], dtype=jnp.int32) - leading
    return jnp.zeros_like(expert).at[ordering].set(position)

def dispatch(rows_x, expert, n_expert, capacity):
    slot_index = slot_table(expert)
    target = expert * capacity + slot_index
    buffer = jnp.zeros((n_expert * capacity, rows_x.shape[1]), rows_x.dtype).at[target].set(rows_x)
    filled = jnp.zeros((n_expert * capacity,), jnp.bfloat16).at[target].set(jnp.ones(expert.shape, jnp.bfloat16))
    return (buffer, filled, target)

def evidence_parts(second_mom, first_mom, counts):
    features = second_mom.shape[-1]
    identity_mat = jnp.eye(features, dtype=jnp.float32)
    kappa_post = 1.0 + counts
    scatter_psi = identity_mat + second_mom - first_mom[..., :, None] * first_mom[..., None, :] / kappa_post[..., None, None]
    factor = jnp.linalg.cholesky(scatter_psi)
    diagonal = jnp.diagonal(factor, axis1=-2, axis2=-1)
    logdet = 2.0 * lax.optimization_barrier(jnp.sum(jnp.log(diagonal), axis=-1))
    prior_dof = features + 3.0
    half_steps = jnp.arange(features, dtype=jnp.float32) * 0.5
    gamma_part = lax.optimization_barrier(jnp.sum(jax.scipy.special.gammaln((prior_dof + counts)[..., None] * 0.5 - half_steps) - jax.scipy.special.gammaln(prior_dof * 0.5 - half_steps), axis=-1))
    evidence = -0.5 * features * math.log(math.pi) * counts + gamma_part - 0.5 * (prior_dof + counts) * logdet - 0.5 * features * jnp.log(kappa_post)
    return (factor, logdet, evidence)

def predictive(factor, logdet, counts, first_mom):
    features = factor.shape[-1]
    identity_mat = jnp.broadcast_to(jnp.eye(features, dtype=jnp.float32), factor.shape)
    inverse = jax.scipy.linalg.solve_triangular(factor, identity_mat, lower=True)
    whiten = jnp.sqrt(counts + 2.0)[..., None, None] * inverse
    center = first_mom / (1.0 + counts)[..., None]
    shifted = jnp.einsum('...fd,...d->...f', whiten, center, precision=HIGH)
    offset = 0.5 * features * jnp.log(counts + 2.0) - 0.5 * logdet
    return (whiten, shifted, offset)

def holder_stats(second_mom, first_mom, counts):
    features = second_mom.shape[-1]
    sub_factor, sub_logdet, sub_evid = evidence_parts(second_mom, first_mom, counts)
    whole_second = second_mom[:, 0] + second_mom[:, 1]
    whole_first = first_mom[:, 0] + first_mom[:, 1]
    whole_counts = counts[:, 0] + counts[:, 1]
    _, _, whole_evid = evidence_parts(whole_second, whole_first, whole_counts)
    whiten, shifted, offset = predictive(sub_factor, sub_logdet, counts, first_mom)
    gammaln = jax.scipy.special.gammaln
    split_score = (sub_evid[:, 0] + sub_evid[:, 1] - whole_evid + gammaln(counts[:, 0]) + gammaln(counts[:, 1]) - gammaln(whole_counts)) / (features * features)
    return (whiten, shifted, offset, split_score, whole_second, whole_first, whole_counts, whole_evid)

def merge_part(own_second, own_first, own_counts, own_evid, mate_second, mate_first, mate_counts, mate_evid):
    features = own_second.shape[-1]
    _, _, merged_evid = evidence_parts(own_second + mate_second, own_first + mate_first, own_counts + mate_counts)
    gammaln = jax.scipy.special.gammaln
    return (merged_evid - own_evid - mate_evid + gammaln(own_counts + mate_counts) - gammaln(own_counts) - gammaln(mate_counts)) / (features * features)

def score_slots(slots, whiten, shifted, offset, logits):
    sources = slots.shape[0]
    groups = min(8, sources)
    grouped = slots.reshape((groups, sources // groups) + slots.shape[1:])

    def one_group(group_rows):
        values = group_rows.astype(jnp.float32)
        image = jnp.einsum('iksad,ktfd->iksatf', values, whiten, precision=HIGH)
        image = image - shifted[None, :, None, None, :, :]
        energy = -0.5 * lax.optimization_barrier(jnp.sum(image * image, axis=-1)) + offset[None, :, None, None, :]
        return jax.nn.sigmoid(logits[None, :, None, None] + energy[..., 1] - energy[..., 0])
    return lax.map(one_group, grouped).reshape(slots.shape[:4])

def reference(embedding, assignment, sub_logit, merge_offset):
    features = embedding.shape[1]
    n_expert = 2 * CLUSTERS
    blocks_x = embedding.reshape(-1, ROW_DEV, features)
    blocks_e = assignment.reshape(-1, ROW_DEV)

    def add_block(carry, inputs):
        rows_x, expert = inputs
        buffer, filled, target = dispatch(rows_x, expert, n_expert, CAP)
        slots = buffer.reshape(n_expert, CAP, features).astype(jnp.float32)
        slot_mask = filled.reshape(n_expert, CAP).astype(jnp.float32)
        second_mom = carry[0] + jnp.einsum('ead,eaf->edf', slots, slots, precision=HIGH)
        first_mom = carry[1] + jnp.einsum('ea,ead->ed', slot_mask, slots, precision=HIGH)
        counts = carry[2] + lax.optimization_barrier(jnp.sum(slot_mask, axis=1))
        return ((second_mom, first_mom, counts), 0)
    start_carry = (jnp.zeros((n_expert, features, features), jnp.float32), jnp.zeros((n_expert, features), jnp.float32), jnp.zeros((n_expert,), jnp.float32))
    (second_mom, first_mom, counts), _ = lax.scan(add_block, start_carry, (blocks_x, blocks_e))
    holder_out = holder_stats(second_mom.reshape(CLUSTERS, 2, features, features), first_mom.reshape(CLUSTERS, 2, features), counts.reshape(CLUSTERS, 2))
    whiten, shifted, offset, split_score = (holder_out[0], holder_out[1], holder_out[2], holder_out[3])

    def score_block(carry, inputs):
        rows_x, expert = inputs
        buffer, filled, target = dispatch(rows_x, expert, n_expert, CAP)
        slots = buffer.reshape(1, CLUSTERS, 2, CAP, features)
        sub_odds = score_slots(slots, whiten, shifted, offset, sub_logit).reshape(-1)
        return (carry, sub_odds[target])
    _, row_probs = lax.scan(score_block, jnp.zeros((), jnp.int32), (blocks_x, blocks_e))
    cluster_ids = jnp.arange(CLUSTERS, dtype=jnp.int32)
    partner = (cluster_ids // K_OWN + merge_offset) % N_OWN * K_OWN + cluster_ids % K_OWN
    merge_score = merge_part(holder_out[4], holder_out[5], holder_out[6], holder_out[7], holder_out[4][partner], holder_out[5][partner], holder_out[6][partner], holder_out[7][partner])
    return (row_probs.reshape(-1), split_score, merge_score)
```

```python
import math

import jax
import jax.numpy as jnp
from jax import lax
from jax.experimental import pallas as pl
from jax.experimental.pallas import tpu as pltpu
from jax.sharding import PartitionSpec as P

D = 128
CAP = 8
EMPTY = 64.0
VMEM_LIMIT = 48 * 1024 * 1024
PANEL = 16


def iota(shape, dim):
    return lax.broadcasted_iota(jnp.int32, shape, dim)


def split3(value):
    high = value.astype(jnp.bfloat16)
    rest = value - high.astype(jnp.float32)
    middle = rest.astype(jnp.bfloat16)
    low = (rest - middle.astype(jnp.float32)).astype(jnp.bfloat16)
    return high, middle, low


def slots_of(labels):
    blocks = labels.shape[0]
    flipped = jnp.transpose(labels.astype(jnp.float32))
    before = iota((128, 128), 0) < iota((128, 128), 1)
    lanes = iota((128, 128), 1)
    levels = iota((8, 128), 0)
    running = jnp.zeros((8, 128), jnp.float32)
    rows = []
    for b in range(blocks):
        across = labels[b : b + 1, :]
        down = jnp.broadcast_to(flipped[:, b : b + 1], (128, 128)).astype(jnp.int32)
        same = jnp.where((down == across) & before, 1.0, 0.0)
        inside = jnp.sum(same, axis=0, keepdims=True)
        low = across & 127
        upper = levels == (across >> 7)
        found = jnp.take_along_axis(running, jnp.broadcast_to(low, (8, 128)), axis=1)
        earlier = jnp.sum(jnp.where(upper, found, 0.0), axis=0, keepdims=True)
        rows.append(across * CAP + (inside + earlier).astype(jnp.int32))
        hot_low = jnp.where((down & 127) == lanes, 1.0, 0.0).astype(jnp.bfloat16)
        hot_up = jnp.where(upper, 1.0, 0.0).astype(jnp.bfloat16)
        running = running + jnp.dot(hot_up, hot_low, preferred_element_type=jnp.float32)
    return jnp.concatenate(rows, axis=0)


def dispatch_kernel(labels_ref, rows_ref, target_ref, out_ref, wide, table, places, sem):
    target_ref[...] = slots_of(labels_ref[...])
    copy = pltpu.make_async_copy(target_ref, places, sem)
    copy.start()
    wide[...] = rows_ref[...].astype(jnp.float32)
    table[...] = jnp.full(table.shape, EMPTY, jnp.float32)
    copy.wait()

    def block(b, carry):
        for j in range(128):
            table[pl.ds(places[b, j], 1), :] = wide[pl.ds(b * 128 + j, 1), :]
        return carry

    lax.fori_loop(0, labels_ref.shape[0], block, 0)
    out_ref[...] = table[...].astype(jnp.bfloat16)


def dispatch(embedding, labels, slots):
    total = embedding.shape[0]
    return pl.pallas_call(
        dispatch_kernel,
        out_shape=(
            jax.ShapeDtypeStruct(labels.shape, jnp.int32),
            jax.ShapeDtypeStruct((slots, D), jnp.bfloat16),
        ),
        in_specs=[pl.BlockSpec(memory_space=pltpu.VMEM)] * 2,
        out_specs=[pl.BlockSpec(memory_space=pltpu.VMEM)] * 2,
        scratch_shapes=[
            pltpu.VMEM((total, D), jnp.float32),
            pltpu.VMEM((slots, D), jnp.float32),
            pltpu.SMEM(labels.shape, jnp.int32),
            pltpu.SemaphoreType.DMA,
        ],
        compiler_params=pltpu.CompilerParams(vmem_limit_bytes=VMEM_LIMIT),
    )(labels, embedding)


def eliminate(work, count):
    pivots = [[] for _ in range(count)]
    lanes = iota((PANEL, D), 1)
    down = iota((PANEL, D), 0)
    for p in range(D // PANEL):
        base = p * PANEL
        tiles = [work[m, base : base + PANEL, :] for m in range(count)]
        diag = [jnp.ones((PANEL, D), jnp.float32) for _ in range(count)]
        for i in range(PANEL):
            j = base + i
            at_col = lanes == j
            for m in range(count):
                tile = tiles[m]
                column = jnp.broadcast_to(tile[:, j : j + 1], (PANEL, D))
                pivot = column[i : i + 1, :]
                factor = jnp.where(down > i, column * (1.0 / pivot), 0.0)
                diag[m] = jnp.where(down == i, pivot, diag[m])
                edge = jnp.where(down == i, 1.0, -factor)
                tiles[m] = jnp.where(at_col, edge, tile - factor * tile[i : i + 1, :])
        for m in range(count):
            pivots[m].append(diag[m])
            work[m, base : base + PANEL, :] = tiles[m]
            below = base + PANEL
            if below < D:
                e1, e2, e3 = split3(tiles[m])
                n1, n2, n3 = split3(tiles[m] * (1.0 / diag[m]))
                left = jnp.concatenate([n1, n1, n2, n2, n1, n3], axis=0)
                right = jnp.concatenate([e1, e2, e1, e2, e3, e1], axis=0)
                step = lax.dot_general(
                    left,
                    right,
                    (((0,), (0,)), ((), ())),
                    preferred_element_type=jnp.float32,
                )
                old = work[m, below:, :]
                wide_lanes = iota(old.shape, 1)
                inside = (wide_lanes >= base) & (wide_lanes < below)
                work[m, below:, :] = jnp.where(inside, 0.0, old) - step[below:, :]
    return pivots


def log_sum(pivot_tiles):
    total = jnp.zeros((1, D), jnp.float32)
    for tile in pivot_tiles:
        total = total + jnp.sum(jnp.log(tile), axis=0, keepdims=True)
    return total


def posterior_scatter(second, first, number):
    same = iota((D, D), 0) == iota((D, D), 1)
    over = jnp.broadcast_to(first, (D, D))
    return jnp.where(same, 1.0, 0.0) + second - jnp.transpose(over) * over / (1.0 + number)


def factor_kernel(logit_ref, rows_ref, xt_ref, maps_ref, shift_ref, const_ref, pack_ref, info_ref, work):
    sources = rows_ref.shape[0]
    depth = sources * 16
    moments = []
    for c in range(2):
        rows = rows_ref[:, 16 * c : 16 * c + 16, :].reshape(depth, D)
        empty = rows.astype(jnp.float32) > 8.0
        clean = jnp.where(empty, 0.0, rows.astype(jnp.float32)).astype(jnp.bfloat16)
        valid = jnp.where(empty, 0.0, 1.0).astype(jnp.bfloat16)
        turned = jnp.transpose(clean)
        xt_ref[c] = turned
        zero_side = (iota((D, depth), 1) & 8) == 0
        none = jnp.zeros_like(turned)
        left = jnp.concatenate(
            [jnp.where(zero_side, turned, none), jnp.where(zero_side, none, turned)], axis=0
        )
        second = jnp.dot(left, clean, preferred_element_type=jnp.float32)
        side = ((iota((16, depth), 1) >> 3) & 1) == (iota((16, depth), 0) & 1)
        pick = jnp.where(side, 1.0, 0.0).astype(jnp.bfloat16)
        first = jnp.dot(pick, clean, preferred_element_type=jnp.float32)
        number = jnp.dot(pick, valid, preferred_element_type=jnp.float32)
        for s in range(2):
            moments.append((second[s * D : (s + 1) * D], first[s : s + 1], number[s : s + 1]))
    for c in range(2):
        moments.append(tuple(a + b for a, b in zip(moments[2 * c], moments[2 * c + 1])))
    for m in range(6):
        work[m] = posterior_scatter(*moments[m])
    lower = iota((D, D), 0) >= iota((D, D), 1)
    same = iota((D, D), 0) == iota((D, D), 1)
    pack_ref[0:D, :] = jnp.where(lower, moments[4][0], moments[5][0])
    diagonal = jnp.sum(jnp.where(same, moments[5][0], 0.0), axis=0, keepdims=True)

    pivots = eliminate(work, 6)

    logdets = [log_sum(tiles) for tiles in pivots]
    tail = [diagonal, moments[4][1], moments[5][1], moments[4][2], moments[5][2]]
    pack_ref[D : D + 8, :] = jnp.concatenate(
        tail + [logdets[4], logdets[5], jnp.zeros((1, D), jnp.float32)], axis=0
    )
    info_ref[...] = jnp.concatenate(
        [moments[m][2] for m in range(4)] + logdets[:4], axis=0
    )
    for c in range(2):
        offsets = []
        for t in range(2):
            m = 2 * c + t
            _, first, number = moments[m]
            spread = jnp.concatenate(pivots[m], axis=0)
            unit = jnp.where(lower, work[m], 0.0)
            whiten = jnp.sqrt(number + 2.0) * (unit * lax.rsqrt(spread))
            center = first / (1.0 + number)
            shifted = jnp.sum(whiten * center, axis=1, keepdims=True)
            shift_ref[c, t * D : (t + 1) * D, :] = jnp.broadcast_to(shifted, (D, D))
            for k, piece in enumerate(split3(whiten)):
                maps_ref[c, k, t * D : (t + 1) * D, :] = piece
            offsets.append(0.5 * D * jnp.log(number + 2.0) - 0.5 * logdets[m])
        const_ref[c] = jnp.broadcast_to(logit_ref[c] + (offsets[1] - offsets[0]), (8, D))


def factor(logits, arrived):
    sources = arrived.shape[0]
    depth = sources * 16
    f32 = jnp.float32
    return pl.pallas_call(
        factor_kernel,
        out_shape=(
            jax.ShapeDtypeStruct((2, D, depth), jnp.bfloat16),
            jax.ShapeDtypeStruct((2, 3, 2 * D, D), jnp.bfloat16),
            jax.ShapeDtypeStruct((2, 2 * D, D), f32),
            jax.ShapeDtypeStruct((2, 8, D), f32),
            jax.ShapeDtypeStruct((D + 8, D), f32),
            jax.ShapeDtypeStruct((8, D), f32),
        ),
        in_specs=[
            pl.BlockSpec(memory_space=pltpu.SMEM),
            pl.BlockSpec(memory_space=pltpu.VMEM),
        ],
        out_specs=[pl.BlockSpec(memory_space=pltpu.VMEM)] * 6,
        scratch_shapes=[pltpu.VMEM((6, D, D), f32)],
        compiler_params=pltpu.CompilerParams(vmem_limit_bytes=VMEM_LIMIT),
    )(logits, arrived)


def score_kernel(xt_ref, maps_ref, shift_ref, const_ref, out_ref):
    columns = xt_ref[...]
    image = jnp.dot(maps_ref[2], columns, preferred_element_type=jnp.float32)
    image = image + jnp.dot(maps_ref[1], columns, preferred_element_type=jnp.float32)
    image = image + jnp.dot(maps_ref[0], columns, preferred_element_type=jnp.float32)
    image = image - shift_ref[:, 0:1]
    squares = image * image
    total0 = jnp.sum(squares[:D], axis=0, keepdims=True)
    total1 = jnp.sum(squares[D:], axis=0, keepdims=True)
    odds = const_ref[0:1, 0:1] + 0.5 * (total0 - total1)
    out_ref[...] = 1.0 / (1.0 + jnp.exp(-odds))


def score(xt, maps, shift, const):
    clusters, _, depth = xt.shape
    width = min(512, depth)
    return pl.pallas_call(
        score_kernel,
        out_shape=jax.ShapeDtypeStruct((clusters, 1, depth), jnp.float32),
        grid=(clusters, depth // width),
        in_specs=[
            pl.BlockSpec((None, D, width), lambda c, w: (c, 0, w)),
            pl.BlockSpec((None, 3, 2 * D, D), lambda c, w: (c, 0, 0, 0)),
            pl.BlockSpec((None, 2 * D, D), lambda c, w: (c, 0, 0)),
            pl.BlockSpec((None, 8, D), lambda c, w: (c, 0, 0)),
        ],
        out_specs=pl.BlockSpec((None, 1, width), lambda c, w: (c, 0, w)),
        compiler_params=pltpu.CompilerParams(vmem_limit_bytes=VMEM_LIMIT),
    )(xt, maps, shift, const)


def unpack(pack):
    body = pack[0:D]
    flipped = jnp.transpose(body)
    low = iota((D, D), 0) > iota((D, D), 1)
    same = iota((D, D), 0) == iota((D, D), 1)
    second0 = jnp.where(low, body, flipped)
    second1 = jnp.where(same, pack[D : D + 1], jnp.where(low, flipped, body))
    return (
        (second0, pack[D + 1 : D + 2], pack[D + 3 : D + 4], pack[D + 5 : D + 6]),
        (second1, pack[D + 2 : D + 3], pack[D + 4 : D + 5], pack[D + 6 : D + 7]),
    )


def merge_kernel(mate_ref, own_ref, mate0_ref, mate1_ref, out_ref, work):
    own = unpack(own_ref[...])
    mates = (unpack(mate0_ref[...])[0], unpack(mate1_ref[...])[1])
    for c in range(2):
        work[c] = posterior_scatter(*(own[c][k] + mates[c][k] for k in range(3)))
    pivots = eliminate(work, 2)
    out_ref[...] = jnp.concatenate(
        [mates[c][2] for c in range(2)]
        + [mates[c][3] for c in range(2)]
        + [log_sum(pivots[c]) for c in range(2)]
        + [jnp.zeros((2, D), jnp.float32)],
        axis=0,
    )


def merge(mate, own, everyone):
    block = (None,) + own.shape
    return pl.pallas_call(
        merge_kernel,
        out_shape=jax.ShapeDtypeStruct((8, D), jnp.float32),
        grid_spec=pltpu.PrefetchScalarGridSpec(
            num_scalar_prefetch=1,
            grid=(1,),
            in_specs=[
                pl.BlockSpec(own.shape, lambda g, mate: (0, 0)),
                pl.BlockSpec(block, lambda g, mate: (mate[0], 0, 0)),
                pl.BlockSpec(block, lambda g, mate: (mate[1], 0, 0)),
            ],
            out_specs=pl.BlockSpec((8, D), lambda g, mate: (0, 0)),
            scratch_shapes=[pltpu.VMEM((2, D, D), jnp.float32)],
        ),
        compiler_params=pltpu.CompilerParams(vmem_limit_bytes=VMEM_LIMIT),
    )(mate, own, everyone, everyone)


def read_kernel(table_ref, target_ref, out_ref):
    target = target_ref[...]
    upper = target >> 7
    low = target & 127
    for g in range(target.shape[0] // 8):
        part = slice(8 * g, 8 * g + 8)
        total = jnp.zeros((8, 128), jnp.float32)
        for k in range(table_ref.shape[0]):
            line = jnp.broadcast_to(table_ref[k : k + 1, :], (8, 128))
            found = jnp.take_along_axis(line, low[part], axis=1)
            total = jnp.where(upper[part] == k, found, total)
        out_ref[part, :] = total


def read_back(table, target):
    return pl.pallas_call(
        read_kernel,
        out_shape=jax.ShapeDtypeStruct(target.shape, jnp.float32),
    )(table, target)


def evidence(numbers, logdets):
    prior = D + 3.0
    half_steps = jnp.arange(D, dtype=jnp.float32) * 0.5
    gammaln = jax.scipy.special.gammaln
    gamma_part = jnp.sum(
        gammaln((prior + numbers)[:, None] * 0.5 - half_steps) - gammaln(prior * 0.5 - half_steps),
        axis=-1,
    )
    return (
        -0.5 * D * math.log(math.pi) * numbers
        + gamma_part
        - 0.5 * (prior + numbers) * logdets
        - 0.5 * D * jnp.log(1.0 + numbers)
    )


def scores(info, pack, merged):
    sub_n, sub_logdet = info[0:4, 0], info[4:8, 0]
    whole_n, whole_logdet = pack[D + 3 : D + 5, 0], pack[D + 5 : D + 7, 0]
    mate_n, mate_logdet, both_logdet = merged[0:2, 0], merged[2:4, 0], merged[4:6, 0]
    numbers = jnp.concatenate([sub_n, whole_n, mate_n, whole_n + mate_n])
    logdets = jnp.concatenate([sub_logdet, whole_logdet, mate_logdet, both_logdet])
    value = evidence(numbers, logdets)
    value = value + jax.scipy.special.gammaln(numbers)
    split = (value[0:4].reshape(2, 2).sum(axis=1) - value[4:6]) / (D * D)
    join = (value[8:10] - value[4:6] - value[6:8]) / (D * D)
    return split, join


def shards(embedding, assignment, sub_logit, merge_offset):
    owners, holders = lax.axis_size("own"), lax.axis_size("rows")
    experts = 2 * owners * sub_logit.shape[0]
    axes = ("own", "rows")
    devices = owners * holders
    labels = assignment.reshape(-1, 128)
    target, outgoing = dispatch(embedding, labels, experts * CAP)
    per_holder = merge_offset.shape[0]
    chunk = 2 * per_holder * CAP
    arrived = lax.all_to_all(
        outgoing.reshape(devices, chunk, D), axes, split_axis=0, concat_axis=0, tiled=True
    )
    logits = lax.dynamic_slice(sub_logit, (lax.axis_index("rows") * per_holder,), (per_holder,))
    xt, maps, shift, const, pack, info = factor(logits, arrived)
    everyone = lax.all_gather(pack, "own", axis=0, tiled=False)
    odds = score(xt, maps, shift, const)
    outward = odds.reshape(per_holder, devices, 2 * CAP).transpose(1, 0, 2).reshape(devices, chunk)
    returned = lax.all_to_all(outward, axes, split_axis=0, concat_axis=0, tiled=True)
    mate = (lax.axis_index("own") + merge_offset) % owners
    merged = merge(mate, pack, everyone)
    split, join = scores(info, pack, merged)
    sub_prob = read_back(returned.reshape(-1, 128), target).reshape(-1)
    return (sub_prob, split, join)


def solution(mesh):
    in_specs = (P(("rows", "own"), None), P(("rows", "own"), None), P("own"), P(("own", "rows")))
    out_specs = (P(("rows", "own")), P(("own", "rows")), P(("own", "rows")))
    return jax.shard_map(shards, mesh=mesh, in_specs=in_specs, out_specs=out_specs, check_vma=False)
```

```python
import math

import jax
import jax.numpy as jnp
from jax import lax
from jax.experimental import pallas as pl
from jax.experimental.pallas import tpu as pltpu
from jax.sharding import PartitionSpec as P

D = 128
CAP = 8
EMPTY = 64.0
VMEM_LIMIT = 48 * 1024 * 1024
DISPATCH_LIMIT = 60 * 1024 * 1024
PANEL = 16
STEP = 4
PIECES = 4


def iota(shape, dim):
    return lax.broadcasted_iota(jnp.int32, shape, dim)


def split3(value):
    high = value.astype(jnp.bfloat16)
    rest = value - high.astype(jnp.float32)
    middle = rest.astype(jnp.bfloat16)
    low = (rest - middle.astype(jnp.float32)).astype(jnp.bfloat16)
    return high, middle, low


def slots_of(labels):
    blocks = labels.shape[0]
    flipped = jnp.transpose(labels.astype(jnp.float32))
    before = iota((128, 128), 0) < iota((128, 128), 1)
    lanes = iota((128, 128), 1)
    levels = iota((8, 128), 0)
    running = jnp.zeros((8, 128), jnp.float32)
    rows = []
    for b in range(blocks):
        across = labels[b : b + 1, :]
        down = jnp.broadcast_to(flipped[:, b : b + 1], (128, 128)).astype(jnp.int32)
        same = jnp.where((down == across) & before, 1.0, 0.0)
        inside = jnp.sum(same, axis=0, keepdims=True)
        low = across & 127
        upper = levels == (across >> 7)
        found = jnp.take_along_axis(running, jnp.broadcast_to(low, (8, 128)), axis=1)
        earlier = jnp.sum(jnp.where(upper, found, 0.0), axis=0, keepdims=True)
        rows.append(across * CAP + (inside + earlier).astype(jnp.int32))
        hot_low = jnp.where((down & 127) == lanes, 1.0, 0.0).astype(jnp.bfloat16)
        hot_up = jnp.where(upper, 1.0, 0.0).astype(jnp.bfloat16)
        running = running + jnp.dot(hot_up, hot_low, preferred_element_type=jnp.float32)
    return jnp.concatenate(rows, axis=0)


def dispatch_kernel(labels_ref, rows_ref, target_ref, out_ref, held, rows, wide, table, ready, places, sems):
    load_labels = pltpu.make_async_copy(labels_ref, held, sems.at[0])
    load_labels.start()
    load_rows = pltpu.make_async_copy(rows_ref, rows, sems.at[1])
    load_rows.start()
    table[...] = jnp.full(table.shape, EMPTY, jnp.float32)
    load_labels.wait()
    target_ref[...] = slots_of(held[...])
    copy = pltpu.make_async_copy(target_ref, places, sems.at[2])
    copy.start()
    load_rows.wait()
    wide[...] = rows[...].astype(jnp.float32)
    copy.wait()

    def block(b, carry):
        for j in range(128):
            table[pl.ds(places[b, j], 1), :] = wide[pl.ds(b * 128 + j, 1), :]
        return carry

    lax.fori_loop(0, held.shape[0], block, 0)
    piece = table.shape[0] // PIECES
    stores = []
    for k in range(PIECES):
        part = pl.ds(k * piece, piece)
        ready[part, :] = table[part, :].astype(jnp.bfloat16)
        stores.append(pltpu.make_async_copy(ready.at[part], out_ref.at[part], sems.at[3 + k]))
        stores[-1].start()
    for store in stores:
        store.wait()


def dispatch(embedding, labels, slots):
    total = embedding.shape[0]
    return pl.pallas_call(
        dispatch_kernel,
        out_shape=(
            jax.ShapeDtypeStruct(labels.shape, jnp.int32),
            jax.ShapeDtypeStruct((slots, D), jnp.bfloat16),
        ),
        in_specs=[pl.BlockSpec(memory_space=pltpu.HBM)] * 2,
        out_specs=[
            pl.BlockSpec(memory_space=pltpu.VMEM),
            pl.BlockSpec(memory_space=pltpu.HBM),
        ],
        scratch_shapes=[
            pltpu.VMEM(labels.shape, jnp.int32),
            pltpu.VMEM((total, D), jnp.bfloat16),
            pltpu.VMEM((total, D), jnp.float32),
            pltpu.VMEM((slots, D), jnp.float32),
            pltpu.VMEM((slots, D), jnp.bfloat16),
            pltpu.SMEM(labels.shape, jnp.int32),
            pltpu.SemaphoreType.DMA((3 + PIECES,)),
        ],
        compiler_params=pltpu.CompilerParams(vmem_limit_bytes=DISPATCH_LIMIT),
    )(labels, embedding)


def eliminate(work, count):
    pivots = [[] for _ in range(count)]
    lanes = iota((PANEL, D), 1)
    down = iota((PANEL, D), 0)
    for p in range(D // PANEL):
        base = p * PANEL
        tiles = [work[m, base : base + PANEL, :] for m in range(count)]
        diag = [jnp.ones((PANEL, D), jnp.float32) for _ in range(count)]
        for i in range(0, PANEL, STEP):
            inside = (lanes >= base + i) & (lanes < base + i + STEP)
            unit = jnp.where(lanes - base == down, 1.0, 0.0)
            for m in range(count):
                tile = tiles[m]
                columns = [
                    jnp.broadcast_to(tile[:, base + i + t : base + i + t + 1], (PANEL, D))
                    for t in range(STEP)
                ]
                small = [
                    [columns[v][i + t : i + t + 1, :] for v in range(STEP)] for t in range(STEP)
                ]
                tile = jnp.where(inside, unit, tile)
                lines = [tile[i + t : i + t + 1, :] for t in range(STEP)]
                for t in range(STEP):
                    inverse = 1.0 / small[t][t]
                    diag[m] = jnp.where(down == i + t, small[t][t], diag[m])
                    for u in range(t + 1, STEP):
                        ratio = small[t][u] * inverse
                        for v in range(u, STEP):
                            small[u][v] = small[u][v] - ratio * small[t][v]
                        columns[u] = columns[u] - ratio * columns[t]
                        lines[u] = lines[u] - ratio * lines[t]
                    factor = jnp.where(down > i + t, columns[t] * inverse, 0.0)
                    tile = tile - factor * lines[t]
                tiles[m] = tile
        for m in range(count):
            pivots[m].append(diag[m])
            work[m, base : base + PANEL, :] = tiles[m]
            below = base + PANEL
            if below < D:
                e1, e2, e3 = split3(tiles[m])
                n1, n2, n3 = split3(tiles[m] * (1.0 / diag[m]))
                left = jnp.concatenate([n1, n1, n2, n2, n1, n3], axis=0)
                right = jnp.concatenate([e1, e2, e1, e2, e3, e1], axis=0)
                step = lax.dot_general(
                    left,
                    right,
                    (((0,), (0,)), ((), ())),
                    preferred_element_type=jnp.float32,
                )
                old = work[m, below:, :]
                wide_lanes = iota(old.shape, 1)
                within = (wide_lanes >= base) & (wide_lanes < below)
                work[m, below:, :] = jnp.where(within, 0.0, old) - step[below:, :]
    return pivots


def log_sum(pivot_tiles):
    total = jnp.zeros((1, D), jnp.float32)
    for tile in pivot_tiles:
        total = total + jnp.sum(jnp.log(tile), axis=0, keepdims=True)
    return total


def posterior_scatter(second, first, number):
    same = iota((D, D), 0) == iota((D, D), 1)
    over = jnp.broadcast_to(first, (D, D))
    return jnp.where(same, 1.0, 0.0) + second - jnp.transpose(over) * over / (1.0 + number)


def moments_kernel(rows_ref, xt_ref, second_ref, info_ref, pack_ref):
    depth = rows_ref.shape[0] * 16
    moments = []
    for c in range(2):
        rows = rows_ref[:, 16 * c : 16 * c + 16, :].reshape(depth, D)
        empty = rows.astype(jnp.float32) > 8.0
        clean = jnp.where(empty, 0.0, rows.astype(jnp.float32)).astype(jnp.bfloat16)
        valid = jnp.where(empty, 0.0, 1.0).astype(jnp.bfloat16)
        turned = jnp.transpose(clean)
        xt_ref[c] = turned
        zero_side = (iota((D, depth), 1) & 8) == 0
        none = jnp.zeros_like(turned)
        left = jnp.concatenate(
            [jnp.where(zero_side, turned, none), jnp.where(zero_side, none, turned)], axis=0
        )
        second = jnp.dot(left, clean, preferred_element_type=jnp.float32)
        side = ((iota((16, depth), 1) >> 3) & 1) == (iota((16, depth), 0) & 1)
        pick = jnp.where(side, 1.0, 0.0).astype(jnp.bfloat16)
        first = jnp.dot(pick, clean, preferred_element_type=jnp.float32)
        number = jnp.dot(pick, valid, preferred_element_type=jnp.float32)
        for s in range(2):
            m = 2 * c + s
            moments.append((second[s * D : (s + 1) * D], first[s : s + 1], number[s : s + 1]))
            second_ref[m] = moments[m][0]
    info_ref[...] = jnp.concatenate(
        [moments[m][1] for m in range(4)] + [moments[m][2] for m in range(4)], axis=0
    )
    whole = [tuple(a + b for a, b in zip(moments[2 * c], moments[2 * c + 1])) for c in range(2)]
    lower = iota((D, D), 0) >= iota((D, D), 1)
    same = iota((D, D), 0) == iota((D, D), 1)
    packed = jnp.where(lower, whole[0][0], whole[1][0])
    diagonal = jnp.sum(jnp.where(same, whole[1][0], 0.0), axis=0, keepdims=True)
    ending = jnp.concatenate(
        [diagonal, whole[0][1], whole[1][1], whole[0][2], whole[1][2], jnp.zeros((3, D), jnp.float32)],
        axis=0,
    )
    for q in range(pack_ref.shape[0]):
        pack_ref[q, 0:D, :] = packed
        pack_ref[q, D : D + 8, :] = ending


def find_moments(arrived, owners):
    depth = arrived.shape[0] * 16
    f32 = jnp.float32
    return pl.pallas_call(
        moments_kernel,
        out_shape=(
            jax.ShapeDtypeStruct((2, D, depth), jnp.bfloat16),
            jax.ShapeDtypeStruct((4, D, D), f32),
            jax.ShapeDtypeStruct((8, D), f32),
            jax.ShapeDtypeStruct((owners, D + 8, D), f32),
        ),
        in_specs=[pl.BlockSpec(memory_space=pltpu.VMEM)],
        out_specs=[pl.BlockSpec(memory_space=pltpu.VMEM)] * 4,
        compiler_params=pltpu.CompilerParams(vmem_limit_bytes=VMEM_LIMIT),
        cost_estimate=pl.CostEstimate(flops=10**9, bytes_accessed=4 * 10**6, transcendentals=0),
    )(arrived)


def judge_kernel(logit_ref, xt_ref, second_ref, info_ref, odds_ref, dets_ref, work, lines):
    clusters, _, depth = xt_ref.shape
    firsts = [info_ref[m : m + 1, :] for m in range(4)]
    numbers = [info_ref[m : m + 1, :] for m in range(4, 8)]
    for m in range(4):
        work[m] = posterior_scatter(second_ref[m], firsts[m], numbers[m])
    pivots = eliminate(work, 4)
    logdets = [log_sum(tiles) for tiles in pivots]
    dets_ref[...] = jnp.concatenate(logdets + numbers, axis=0)
    lower = iota((D, D), 0) >= iota((D, D), 1)
    lanes = iota((depth // 128, 128), 1)
    width = min(512, depth)
    odds = []
    for c in range(clusters):
        offsets, shifts, pieces = [], [], []
        for t in range(2):
            m = 2 * c + t
            spread = jnp.concatenate(pivots[m], axis=0)
            unit = jnp.where(lower, work[m], 0.0)
            whiten = jnp.sqrt(numbers[m] + 2.0) * (unit * lax.rsqrt(spread))
            center = firsts[m] / (1.0 + numbers[m])
            shifted = jnp.sum(whiten * center, axis=1, keepdims=True)
            shifts.append(jnp.broadcast_to(shifted, (D, width)))
            pieces.append(jnp.concatenate(split3(whiten), axis=1))
            offsets.append(0.5 * D * jnp.log(numbers[m] + 2.0) - 0.5 * logdets[m])
        maps = jnp.concatenate(pieces, axis=0)
        shift = jnp.concatenate(shifts, axis=0)
        base = logit_ref[c] + (offsets[1] - offsets[0])
        for w in range(depth // width):
            columns = xt_ref[c, :, w * width : (w + 1) * width]
            image = jnp.dot(
                maps, jnp.concatenate([columns] * 3, axis=0), preferred_element_type=jnp.float32
            )
            image = image - shift
            squares = image * image
            gap = jnp.sum(squares[:D] - squares[D:], axis=0, keepdims=True)
            for v in range(width // 128):
                row = w * (width // 128) + v
                lines[row : row + 1, :] = gap[:, v * 128 : (v + 1) * 128]
        odds.append(1.0 / (1.0 + jnp.exp(-(base + 0.5 * lines[...]))))
    for s in range(8):
        first = pltpu.roll(odds[0], (128 - 16 * s) % 128, 1)
        second = pltpu.roll(odds[1], (144 - 16 * s) % 128, 1)
        odds_ref[pl.ds(s, depth // 128, stride=8), :] = jnp.where(lanes < 16, first, second)


def judge(logits, xt, second, info):
    clusters, _, depth = xt.shape
    f32 = jnp.float32
    return pl.pallas_call(
        judge_kernel,
        out_shape=(
            jax.ShapeDtypeStruct((depth // 16, 128), f32),
            jax.ShapeDtypeStruct((8, D), f32),
        ),
        in_specs=[pl.BlockSpec(memory_space=pltpu.SMEM)]
        + [pl.BlockSpec(memory_space=pltpu.VMEM)] * 3,
        out_specs=[pl.BlockSpec(memory_space=pltpu.VMEM)] * 2,
        scratch_shapes=[pltpu.VMEM((4, D, D), f32), pltpu.VMEM((depth // 128, 128), f32)],
        compiler_params=pltpu.CompilerParams(vmem_limit_bytes=VMEM_LIMIT),
        cost_estimate=pl.CostEstimate(flops=10**10, bytes_accessed=10**7, transcendentals=0),
    )(logits, xt, second, info)


def unpack(pack):
    body = pack[0:D]
    flipped = jnp.transpose(body)
    low = iota((D, D), 0) > iota((D, D), 1)
    same = iota((D, D), 0) == iota((D, D), 1)
    second0 = jnp.where(low, body, flipped)
    second1 = jnp.where(same, pack[D : D + 1], jnp.where(low, flipped, body))
    return (
        (second0, pack[D + 1 : D + 2], pack[D + 3 : D + 4]),
        (second1, pack[D + 2 : D + 3], pack[D + 4 : D + 5]),
    )


def merge_kernel(mate_ref, own_ref, mate0_ref, mate1_ref, out_ref, work):
    own = unpack(own_ref[...])
    mates = (unpack(mate0_ref[...])[0], unpack(mate1_ref[...])[1])
    both = tuple(tuple(a + b for a, b in zip(own[c], mates[c])) for c in range(2))
    stats = own + mates + both
    for m in range(6):
        work[m] = posterior_scatter(*stats[m])
    pivots = eliminate(work, 6)
    blank = [jnp.zeros((2, D), jnp.float32)]
    out_ref[...] = jnp.concatenate(
        [stats[m][2] for m in range(6)] + blank + [log_sum(pivots[m]) for m in range(6)] + blank,
        axis=0,
    )


def merge(mate, own, everyone):
    block = (None,) + own.shape[1:]
    return pl.pallas_call(
        merge_kernel,
        out_shape=jax.ShapeDtypeStruct((16, D), jnp.float32),
        grid_spec=pltpu.PrefetchScalarGridSpec(
            num_scalar_prefetch=1,
            grid=(1,),
            in_specs=[
                pl.BlockSpec(block, lambda g, mate: (0, 0, 0)),
                pl.BlockSpec(block, lambda g, mate: (mate[0], 0, 0)),
                pl.BlockSpec(block, lambda g, mate: (mate[1], 0, 0)),
            ],
            out_specs=pl.BlockSpec((16, D), lambda g, mate: (0, 0)),
            scratch_shapes=[pltpu.VMEM((6, D, D), jnp.float32)],
        ),
        compiler_params=pltpu.CompilerParams(vmem_limit_bytes=VMEM_LIMIT),
        cost_estimate=pl.CostEstimate(flops=8 * 10**9, bytes_accessed=10**6, transcendentals=0),
    )(mate, own, everyone, everyone)


def read_kernel(table_ref, target_ref, out_ref, lines):
    depth = table_ref.shape[0] // 4
    lanes = iota((depth, 128), 1)
    total = table_ref[pl.ds(0, depth, stride=4), 0, :]
    for q in range(1, 4):
        moved = pltpu.roll(table_ref[pl.ds(q, depth, stride=4), 0, :], 32 * q, 1)
        total = jnp.where(lanes >= 32 * q, moved, total)
    lines[...] = total
    target = target_ref[...]
    upper = target >> 7
    low = target & 127
    for g in range(target.shape[0] // 8):
        part = slice(8 * g, 8 * g + 8)
        total = jnp.zeros((8, 128), jnp.float32)
        for k in range(depth):
            line = jnp.broadcast_to(lines[k : k + 1, :], (8, 128))
            found = jnp.take_along_axis(line, low[part], axis=1)
            total = jnp.where(upper[part] == k, found, total)
        out_ref[part, :] = total


def read_back(table, target):
    return pl.pallas_call(
        read_kernel,
        out_shape=jax.ShapeDtypeStruct(target.shape, jnp.float32),
        scratch_shapes=[pltpu.VMEM((table.shape[0] // 4, 128), jnp.float32)],
    )(table, target)


def evidence(numbers, logdets):
    prior = D + 3.0
    half_steps = jnp.arange(D, dtype=jnp.float32) * 0.5
    gammaln = jax.scipy.special.gammaln
    gamma_part = jnp.sum(
        gammaln((prior + numbers)[:, None] * 0.5 - half_steps) - gammaln(prior * 0.5 - half_steps),
        axis=-1,
    )
    return (
        -0.5 * D * math.log(math.pi) * numbers
        + gamma_part
        - 0.5 * (prior + numbers) * logdets
        - 0.5 * D * jnp.log(1.0 + numbers)
    )


def scores(dets, merged):
    numbers = jnp.concatenate([dets[4:8, 0], merged[0:6, 0]])
    logdets = jnp.concatenate([dets[0:4, 0], merged[8:14, 0]])
    value = evidence(numbers, logdets) + jax.scipy.special.gammaln(numbers)
    split = (value[0:4].reshape(2, 2).sum(axis=1) - value[4:6]) / (D * D)
    join = (value[8:10] - value[4:6] - value[6:8]) / (D * D)
    return split, join


def shards(embedding, assignment, sub_logit, merge_offset):
    owners, holders = lax.axis_size("own"), lax.axis_size("rows")
    experts = 2 * owners * sub_logit.shape[0]
    axes = ("own", "rows")
    devices = owners * holders
    labels = assignment.reshape(-1, 128)
    target, outgoing = dispatch(embedding, labels, experts * CAP)
    per_holder = merge_offset.shape[0]
    chunk = 2 * per_holder * CAP
    arrived = lax.all_to_all(
        outgoing.reshape(devices, chunk, D), axes, split_axis=0, concat_axis=0, tiled=True
    )
    logits = lax.dynamic_slice(sub_logit, (lax.axis_index("rows") * per_holder,), (per_holder,))
    xt, second, info, packs = find_moments(arrived, owners)
    everyone = lax.all_to_all(packs, "own", split_axis=0, concat_axis=0, tiled=True)
    odds, dets = judge(logits, xt, second, info)
    odds, everyone = lax.optimization_barrier((odds, everyone))
    returned = lax.all_to_all(
        odds.reshape(devices, 1, 128), axes, split_axis=0, concat_axis=0, tiled=True
    )
    mate = (lax.axis_index("own") + merge_offset) % owners
    merged = merge(mate, packs, everyone)
    split, join = scores(dets, merged)
    sub_prob = read_back(returned, target).reshape(-1)
    return (sub_prob, split, join)


def solution(mesh):
    in_specs = (P(("rows", "own"), None), P(("rows", "own"), None), P("own"), P(("own", "rows")))
    out_specs = (P(("rows", "own")), P(("own", "rows")), P(("own", "rows")))
    return jax.shard_map(shards, mesh=mesh, in_specs=in_specs, out_specs=out_specs, check_vma=False)
```

```python
import math

import jax
import jax.numpy as jnp
from jax import lax
from jax.experimental import pallas as pl
from jax.experimental.pallas import tpu as pltpu
from jax.sharding import PartitionSpec as P

D = 128
CAP = 8
EMPTY = 64.0
VMEM_LIMIT = 48 * 1024 * 1024
WIDE_LIMIT = 60 * 1024 * 1024
MERGE_FLOPS = 1
FAR = 8
NARROW_LIMIT = 16 * 1024 * 1024
PANEL = 16
STEP = 4
PIECES = 4


def iota(shape, dim):
    return lax.broadcasted_iota(jnp.int32, shape, dim)


def split3(value):
    high = value.astype(jnp.bfloat16)
    rest = value - high.astype(jnp.float32)
    middle = rest.astype(jnp.bfloat16)
    low = (rest - middle.astype(jnp.float32)).astype(jnp.bfloat16)
    return high, middle, low


def slots_of(labels):
    blocks = labels.shape[0]
    flipped = jnp.transpose(labels.astype(jnp.float32))
    before = iota((128, 128), 0) < iota((128, 128), 1)
    lanes = iota((128, 128), 1)
    levels = iota((8, 128), 0)
    running = jnp.zeros((8, 128), jnp.float32)
    rows = []
    for b in range(blocks):
        across = labels[b : b + 1, :]
        down = jnp.broadcast_to(flipped[:, b : b + 1], (128, 128)).astype(jnp.int32)
        same = jnp.where((down == across) & before, 1.0, 0.0)
        inside = jnp.sum(same, axis=0, keepdims=True)
        low = across & 127
        upper = levels == (across >> 7)
        found = jnp.take_along_axis(running, jnp.broadcast_to(low, (8, 128)), axis=1)
        earlier = jnp.sum(jnp.where(upper, found, 0.0), axis=0, keepdims=True)
        rows.append(across * CAP + (inside + earlier).astype(jnp.int32))
        hot_low = jnp.where((down & 127) == lanes, 1.0, 0.0).astype(jnp.bfloat16)
        hot_up = jnp.where(upper, 1.0, 0.0).astype(jnp.bfloat16)
        running = running + jnp.dot(hot_up, hot_low, preferred_element_type=jnp.float32)
    return jnp.concatenate(rows, axis=0)


def dispatch_kernel(labels_ref, rows_ref, target_ref, out_ref, held, rows, wide, table, ready, places, sems):
    load_labels = pltpu.make_async_copy(labels_ref, held, sems.at[0])
    load_labels.start()
    load_rows = pltpu.make_async_copy(rows_ref, rows, sems.at[1])
    load_rows.start()
    table[...] = jnp.full(table.shape, EMPTY, jnp.float32)
    load_labels.wait()
    target_ref[...] = slots_of(held[...])
    copy = pltpu.make_async_copy(target_ref, places, sems.at[2])
    copy.start()
    load_rows.wait()
    wide[...] = rows[...].astype(jnp.float32)
    copy.wait()

    def block(b, carry):
        for j in range(128):
            table[pl.ds(places[b, j], 1), :] = wide[pl.ds(b * 128 + j, 1), :]
        return carry

    lax.fori_loop(0, held.shape[0], block, 0)
    piece = table.shape[0] // PIECES
    stores = []
    for k in range(PIECES):
        part = pl.ds(k * piece, piece)
        ready[part, :] = table[part, :].astype(jnp.bfloat16)
        stores.append(pltpu.make_async_copy(ready.at[part], out_ref.at[part], sems.at[3 + k]))
        stores[-1].start()
    for store in stores:
        store.wait()


def dispatch(embedding, labels, slots):
    total = embedding.shape[0]
    return pl.pallas_call(
        dispatch_kernel,
        out_shape=(
            jax.ShapeDtypeStruct(labels.shape, jnp.int32),
            jax.ShapeDtypeStruct((slots, D), jnp.bfloat16),
        ),
        in_specs=[pl.BlockSpec(memory_space=pltpu.HBM)] * 2,
        out_specs=[
            pl.BlockSpec(memory_space=pltpu.VMEM),
            pl.BlockSpec(memory_space=pltpu.HBM),
        ],
        scratch_shapes=[
            pltpu.VMEM(labels.shape, jnp.int32),
            pltpu.VMEM((total, D), jnp.bfloat16),
            pltpu.VMEM((total, D), jnp.float32),
            pltpu.VMEM((slots, D), jnp.float32),
            pltpu.VMEM((slots, D), jnp.bfloat16),
            pltpu.SMEM(labels.shape, jnp.int32),
            pltpu.SemaphoreType.DMA((3 + PIECES,)),
        ],
        compiler_params=pltpu.CompilerParams(vmem_limit_bytes=WIDE_LIMIT),
    )(labels, embedding)


def eliminate(work, count):
    pivots = [[] for _ in range(count)]
    lanes = iota((PANEL, D), 1)
    down = iota((PANEL, D), 0)
    for p in range(D // PANEL):
        base = p * PANEL
        tiles = [work[m, base : base + PANEL, :] for m in range(count)]
        diag = [jnp.ones((PANEL, D), jnp.float32) for _ in range(count)]
        for i in range(0, PANEL, STEP):
            inside = (lanes >= base + i) & (lanes < base + i + STEP)
            unit = jnp.where(lanes - base == down, 1.0, 0.0)
            for m in range(count):
                tile = tiles[m]
                columns = [
                    jnp.broadcast_to(tile[:, base + i + t : base + i + t + 1], (PANEL, D))
                    for t in range(STEP)
                ]
                small = [
                    [columns[v][i + t : i + t + 1, :] for v in range(STEP)] for t in range(STEP)
                ]
                tile = jnp.where(inside, unit, tile)
                lines = [tile[i + t : i + t + 1, :] for t in range(STEP)]
                for t in range(STEP):
                    inverse = 1.0 / small[t][t]
                    diag[m] = jnp.where(down == i + t, small[t][t], diag[m])
                    for u in range(t + 1, STEP):
                        ratio = small[t][u] * inverse
                        for v in range(u, STEP):
                            small[u][v] = small[u][v] - ratio * small[t][v]
                        columns[u] = columns[u] - ratio * columns[t]
                        lines[u] = lines[u] - ratio * lines[t]
                    factor = jnp.where(down > i + t, columns[t] * inverse, 0.0)
                    tile = tile - factor * lines[t]
                tiles[m] = tile
        for m in range(count):
            pivots[m].append(diag[m])
            work[m, base : base + PANEL, :] = tiles[m]
            below = base + PANEL
            if below < D:
                e1, e2, e3 = split3(tiles[m])
                n1, n2, n3 = split3(tiles[m] * (1.0 / diag[m]))
                left = jnp.concatenate([n1, n1, n2, n2, n1, n3], axis=0)
                right = jnp.concatenate([e1, e2, e1, e2, e3, e1], axis=0)
                step = lax.dot_general(
                    left,
                    right,
                    (((0,), (0,)), ((), ())),
                    preferred_element_type=jnp.float32,
                )
                old = work[m, below:, :]
                wide_lanes = iota(old.shape, 1)
                within = (wide_lanes >= base) & (wide_lanes < below)
                work[m, below:, :] = jnp.where(within, 0.0, old) - step[below:, :]
    return pivots


def log_sum(pivot_tiles):
    total = jnp.zeros((1, D), jnp.float32)
    for tile in pivot_tiles:
        total = total + jnp.sum(jnp.log(tile), axis=0, keepdims=True)
    return total


def posterior_scatter(second, first, number):
    same = iota((D, D), 0) == iota((D, D), 1)
    over = jnp.broadcast_to(first, (D, D))
    return jnp.where(same, 1.0, 0.0) + second - jnp.transpose(over) * over / (1.0 + number)


def moments_kernel(rows_ref, xt_ref, second_ref, info_ref, pack_ref, turned_ref, sems):
    stores = []
    depth = rows_ref.shape[0] * 16
    moments = []
    for c in range(2):
        rows = rows_ref[:, 16 * c : 16 * c + 16, :].reshape(depth, D)
        empty = rows.astype(jnp.float32) > 8.0
        clean = jnp.where(empty, 0.0, rows.astype(jnp.float32)).astype(jnp.bfloat16)
        valid = jnp.where(empty, 0.0, 1.0).astype(jnp.bfloat16)
        turned = jnp.transpose(clean)
        turned_ref[c] = turned
        stores.append(pltpu.make_async_copy(turned_ref.at[c], xt_ref.at[c], sems.at[c]))
        stores[c].start()
        zero_side = (iota((D, depth), 1) & 8) == 0
        none = jnp.zeros_like(turned)
        left = jnp.concatenate(
            [jnp.where(zero_side, turned, none), jnp.where(zero_side, none, turned)], axis=0
        )
        second = jnp.dot(left, clean, preferred_element_type=jnp.float32)
        side = ((iota((16, depth), 1) >> 3) & 1) == (iota((16, depth), 0) & 1)
        pick = jnp.where(side, 1.0, 0.0).astype(jnp.bfloat16)
        first = jnp.dot(pick, clean, preferred_element_type=jnp.float32)
        number = jnp.dot(pick, valid, preferred_element_type=jnp.float32)
        for s in range(2):
            m = 2 * c + s
            moments.append((second[s * D : (s + 1) * D], first[s : s + 1], number[s : s + 1]))
            second_ref[m] = moments[m][0]
    info_ref[...] = jnp.concatenate(
        [moments[m][1] for m in range(4)] + [moments[m][2] for m in range(4)], axis=0
    )
    whole = [tuple(a + b for a, b in zip(moments[2 * c], moments[2 * c + 1])) for c in range(2)]
    lower = iota((D, D), 0) >= iota((D, D), 1)
    same = iota((D, D), 0) == iota((D, D), 1)
    packed = jnp.where(lower, whole[0][0], whole[1][0])
    diagonal = jnp.sum(jnp.where(same, whole[1][0], 0.0), axis=0, keepdims=True)
    ending = jnp.concatenate(
        [diagonal, whole[0][1], whole[1][1], whole[0][2], whole[1][2], jnp.zeros((3, D), jnp.float32)],
        axis=0,
    )
    for q in range(pack_ref.shape[0]):
        pack_ref[q, 0:D, :] = packed
        pack_ref[q, D : D + 8, :] = ending
    for store in stores:
        store.wait()


def find_moments(arrived, owners):
    depth = arrived.shape[0] * 16
    f32 = jnp.float32
    return pl.pallas_call(
        moments_kernel,
        out_shape=(
            jax.ShapeDtypeStruct((FAR, D, depth), jnp.bfloat16),
            jax.ShapeDtypeStruct((4, D, D), f32),
            jax.ShapeDtypeStruct((8, D), f32),
            jax.ShapeDtypeStruct((owners, D + 8, D), f32),
        ),
        in_specs=[pl.BlockSpec(memory_space=pltpu.VMEM)],
        out_specs=[pl.BlockSpec(memory_space=pltpu.HBM)]
        + [pl.BlockSpec(memory_space=pltpu.VMEM)] * 3,
        scratch_shapes=[
            pltpu.VMEM((2, D, depth), jnp.bfloat16),
            pltpu.SemaphoreType.DMA((2,)),
        ],
        compiler_params=pltpu.CompilerParams(vmem_limit_bytes=VMEM_LIMIT),
        cost_estimate=pl.CostEstimate(flops=10**9, bytes_accessed=4 * 10**6, transcendentals=0),
    )(arrived)


def judge_kernel(logit_ref, far_ref, second_ref, info_ref, odds_ref, dets_ref, work, lines, xt_ref, sem):
    load = pltpu.make_async_copy(far_ref.at[0:2], xt_ref, sem)
    load.start()
    clusters, _, depth = xt_ref.shape
    firsts = [info_ref[m : m + 1, :] for m in range(4)]
    numbers = [info_ref[m : m + 1, :] for m in range(4, 8)]
    for m in range(4):
        work[m] = posterior_scatter(second_ref[m], firsts[m], numbers[m])
    pivots = eliminate(work, 4)
    logdets = [log_sum(tiles) for tiles in pivots]
    dets_ref[...] = jnp.concatenate(logdets + numbers, axis=0)
    lower = iota((D, D), 0) >= iota((D, D), 1)
    lanes = iota((depth // 128, 128), 1)
    width = min(512, depth)
    odds = []
    load.wait()
    for c in range(clusters):
        offsets, shifts, pieces = [], [], []
        for t in range(2):
            m = 2 * c + t
            spread = jnp.concatenate(pivots[m], axis=0)
            unit = jnp.where(lower, work[m], 0.0)
            whiten = jnp.sqrt(numbers[m] + 2.0) * (unit * lax.rsqrt(spread))
            center = firsts[m] / (1.0 + numbers[m])
            shifted = jnp.sum(whiten * center, axis=1, keepdims=True)
            shifts.append(jnp.broadcast_to(shifted, (D, width)))
            pieces.append(jnp.concatenate(split3(whiten), axis=1))
            offsets.append(0.5 * D * jnp.log(numbers[m] + 2.0) - 0.5 * logdets[m])
        maps = jnp.concatenate(pieces, axis=0)
        shift = jnp.concatenate(shifts, axis=0)
        base = logit_ref[c] + (offsets[1] - offsets[0])
        for w in range(depth // width):
            columns = xt_ref[c, :, w * width : (w + 1) * width]
            image = jnp.dot(
                maps, jnp.concatenate([columns] * 3, axis=0), preferred_element_type=jnp.float32
            )
            image = image - shift
            squares = image * image
            gap = jnp.sum(squares[:D] - squares[D:], axis=0, keepdims=True)
            for v in range(width // 128):
                row = w * (width // 128) + v
                lines[row : row + 1, :] = gap[:, v * 128 : (v + 1) * 128]
        odds.append(1.0 / (1.0 + jnp.exp(-(base + 0.5 * lines[...]))))
    for s in range(8):
        first = pltpu.roll(odds[0], (128 - 16 * s) % 128, 1)
        second = pltpu.roll(odds[1], (144 - 16 * s) % 128, 1)
        odds_ref[pl.ds(s, depth // 128, stride=8), :] = jnp.where(lanes < 16, first, second)


def judge(logits, xt, second, info):
    depth = xt.shape[2]
    f32 = jnp.float32
    return pl.pallas_call(
        judge_kernel,
        out_shape=(
            jax.ShapeDtypeStruct((depth // 16, 128), f32),
            jax.ShapeDtypeStruct((8, D), f32),
        ),
        in_specs=[
            pl.BlockSpec(memory_space=pltpu.SMEM),
            pl.BlockSpec(memory_space=pltpu.HBM),
            pl.BlockSpec(memory_space=pltpu.VMEM),
            pl.BlockSpec(memory_space=pltpu.VMEM),
        ],
        out_specs=[pl.BlockSpec(memory_space=pltpu.VMEM)] * 2,
        scratch_shapes=[
            pltpu.VMEM((4, D, D), f32),
            pltpu.VMEM((depth // 128, 128), f32),
            pltpu.VMEM((2, D, depth), jnp.bfloat16),
            pltpu.SemaphoreType.DMA,
        ],
        compiler_params=pltpu.CompilerParams(vmem_limit_bytes=VMEM_LIMIT),
        cost_estimate=pl.CostEstimate(flops=10**10, bytes_accessed=10**7, transcendentals=0),
    )(logits, xt, second, info)


def unpack(pack):
    body = pack[0:D]
    flipped = jnp.transpose(body)
    low = iota((D, D), 0) > iota((D, D), 1)
    same = iota((D, D), 0) == iota((D, D), 1)
    second0 = jnp.where(low, body, flipped)
    second1 = jnp.where(same, pack[D : D + 1], jnp.where(low, flipped, body))
    return (
        (second0, pack[D + 1 : D + 2], pack[D + 3 : D + 4]),
        (second1, pack[D + 2 : D + 3], pack[D + 4 : D + 5]),
    )


def log_gamma(x):
    z = x + 8.0
    inverse = 1.0 / z
    square = inverse * inverse
    series = inverse * (1.0 / 12.0 - square * (1.0 / 360.0 - square * (1.0 / 1260.0)))
    low = x * (x + 1.0) * (x + 2.0) * (x + 3.0)
    high = (x + 4.0) * (x + 5.0) * (x + 6.0) * (x + 7.0)
    half_log_tau = 0.5 * math.log(2.0 * math.pi)
    return (z - 0.5) * jnp.log(z) - z + half_log_tau + series - jnp.log(low) - jnp.log(high)


def evidence(numbers, logdets):
    prior = D + 3.0
    half_steps = 0.5 * iota(numbers.shape, 1).astype(jnp.float32)
    terms = log_gamma(0.5 * (prior + numbers) - half_steps) - log_gamma(0.5 * prior - half_steps)
    return (
        -0.5 * D * math.log(math.pi) * numbers
        + jnp.sum(terms, axis=1, keepdims=True)
        - 0.5 * (prior + numbers) * logdets
        - 0.5 * D * jnp.log(1.0 + numbers)
        + log_gamma(numbers)
    )


def merge_kernel(mate_ref, dets_ref, own_ref, mate0_ref, mate1_ref, split_ref, join_ref, work):
    own = unpack(own_ref[...])
    mates = (unpack(mate0_ref[...])[0], unpack(mate1_ref[...])[1])
    both = tuple(tuple(a + b for a, b in zip(own[c], mates[c])) for c in range(2))
    stats = own + mates + both
    for m in range(6):
        work[m] = posterior_scatter(*stats[m])
    pivots = eliminate(work, 6)
    blank = [jnp.ones((6, D), jnp.float32)]
    numbers = jnp.concatenate([dets_ref[4:8, :]] + [stats[m][2] for m in range(6)] + blank, axis=0)
    logdets = jnp.concatenate([dets_ref[0:4, :]] + [log_sum(pivots[m]) for m in range(6)] + blank, axis=0)
    value = evidence(numbers, logdets)
    for c in range(2):
        whole = value[4 + c : 5 + c]
        split = value[2 * c : 2 * c + 1] + value[2 * c + 1 : 2 * c + 2] - whole
        join = value[8 + c : 9 + c] - whole - value[6 + c : 7 + c]
        split_ref[c] = split[0, 0] * (1.0 / (D * D))
        join_ref[c] = join[0, 0] * (1.0 / (D * D))


def merge(mate, dets, own, everyone):
    block = (None,) + own.shape[1:]
    one = jax.ShapeDtypeStruct((2,), jnp.float32)
    return pl.pallas_call(
        merge_kernel,
        out_shape=(one, one),
        grid_spec=pltpu.PrefetchScalarGridSpec(
            num_scalar_prefetch=1,
            grid=(1,),
            in_specs=[
                pl.BlockSpec(dets.shape, lambda g, mate: (0, 0)),
                pl.BlockSpec(block, lambda g, mate: (0, 0, 0)),
                pl.BlockSpec(block, lambda g, mate: (mate[0], 0, 0)),
                pl.BlockSpec(block, lambda g, mate: (mate[1], 0, 0)),
            ],
            out_specs=[pl.BlockSpec(memory_space=pltpu.SMEM)] * 2,
            scratch_shapes=[pltpu.VMEM((6, D, D), jnp.float32)],
        ),
        compiler_params=pltpu.CompilerParams(vmem_limit_bytes=NARROW_LIMIT),
        cost_estimate=pl.CostEstimate(flops=MERGE_FLOPS, bytes_accessed=1, transcendentals=0),
    )(mate, dets, own, everyone, everyone)


def read_kernel(table_ref, target_ref, out_ref, lines):
    depth = table_ref.shape[0] // 4
    lanes = iota((depth, 128), 1)
    total = table_ref[pl.ds(0, depth, stride=4), 0, :]
    for q in range(1, 4):
        moved = pltpu.roll(table_ref[pl.ds(q, depth, stride=4), 0, :], 32 * q, 1)
        total = jnp.where(lanes >= 32 * q, moved, total)
    lines[...] = total
    target = target_ref[...]
    upper = target >> 7
    low = target & 127
    for g in range(target.shape[0] // 8):
        part = slice(8 * g, 8 * g + 8)
        total = jnp.zeros((8, 128), jnp.float32)
        for k in range(depth):
            line = jnp.broadcast_to(lines[k : k + 1, :], (8, 128))
            found = jnp.take_along_axis(line, low[part], axis=1)
            total = jnp.where(upper[part] == k, found, total)
        out_ref[part, :] = total


def read_back(table, target):
    return pl.pallas_call(
        read_kernel,
        out_shape=jax.ShapeDtypeStruct(target.shape, jnp.float32),
        scratch_shapes=[pltpu.VMEM((table.shape[0] // 4, 128), jnp.float32)],
        compiler_params=pltpu.CompilerParams(vmem_limit_bytes=NARROW_LIMIT),
    )(table, target)


def shards(embedding, assignment, sub_logit, merge_offset):
    owners, holders = lax.axis_size("own"), lax.axis_size("rows")
    experts = 2 * owners * sub_logit.shape[0]
    axes = ("own", "rows")
    devices = owners * holders
    labels = assignment.reshape(-1, 128)
    target, outgoing = dispatch(embedding, labels, experts * CAP)
    per_holder = merge_offset.shape[0]
    chunk = 2 * per_holder * CAP
    arrived = lax.all_to_all(
        outgoing.reshape(devices, chunk, D), axes, split_axis=0, concat_axis=0, tiled=True
    )
    logits = lax.dynamic_slice(sub_logit, (lax.axis_index("rows") * per_holder,), (per_holder,))
    xt, second, info, packs = find_moments(arrived, owners)
    everyone = lax.all_to_all(packs, "own", split_axis=0, concat_axis=0, tiled=True)
    odds, dets = judge(logits, xt, second, info)
    odds, everyone = lax.optimization_barrier((odds, everyone))
    returned = lax.all_to_all(
        odds.reshape(devices, 1, 128), axes, split_axis=0, concat_axis=0, tiled=True
    )
    mate = (lax.axis_index("own") + merge_offset) % owners
    split, join = merge(mate, dets, packs, everyone)
    sub_prob = read_back(returned, target).reshape(-1)
    return (sub_prob, split, join)


def solution(mesh):
    in_specs = (P(("rows", "own"), None), P(("rows", "own"), None), P("own"), P(("own", "rows")))
    out_specs = (P(("rows", "own")), P(("own", "rows")), P(("own", "rows")))
    return jax.shard_map(shards, mesh=mesh, in_specs=in_specs, out_specs=out_specs, check_vma=False)
```

```python
import math

import jax
import jax.numpy as jnp
from jax import lax
from jax.experimental import pallas as pl
from jax.experimental.pallas import tpu as pltpu
from jax.sharding import PartitionSpec as P

D = 128
CAP = 8
EMPTY = 64.0
VMEM_LIMIT = 48 * 1024 * 1024
WIDE_LIMIT = 60 * 1024 * 1024
MERGE_FLOPS = 1
FAR = 8
NARROW_LIMIT = 16 * 1024 * 1024
STEP = 4
PIECES = 4


def iota(shape, dim):
    return lax.broadcasted_iota(jnp.int32, shape, dim)


def split3(value):
    high = value.astype(jnp.bfloat16)
    rest = value - high.astype(jnp.float32)
    middle = rest.astype(jnp.bfloat16)
    low = (rest - middle.astype(jnp.float32)).astype(jnp.bfloat16)
    return high, middle, low


def slots_of(labels, emit):
    blocks = labels.shape[0]
    flipped = jnp.transpose(labels.astype(jnp.float32))
    before = iota((128, 128), 0) < iota((128, 128), 1)
    lanes = iota((128, 128), 1)
    levels = iota((8, 128), 0)
    running = jnp.zeros((8, 128), jnp.float32)
    for b in range(blocks):
        across = labels[b : b + 1, :]
        down = jnp.broadcast_to(flipped[:, b : b + 1], (128, 128)).astype(jnp.int32)
        same = jnp.where((down == across) & before, 1.0, 0.0)
        inside = jnp.sum(same, axis=0, keepdims=True)
        low = across & 127
        upper = levels == (across >> 7)
        found = jnp.take_along_axis(running, jnp.broadcast_to(low, (8, 128)), axis=1)
        earlier = jnp.sum(jnp.where(upper, found, 0.0), axis=0, keepdims=True)
        emit(b, across * CAP + (inside + earlier).astype(jnp.int32))
        hot_low = jnp.where((down & 127) == lanes, 1.0, 0.0).astype(jnp.bfloat16)
        hot_up = jnp.where(upper, 1.0, 0.0).astype(jnp.bfloat16)
        running = running + jnp.dot(hot_up, hot_low, preferred_element_type=jnp.float32)


def dispatch_kernel(labels_ref, rows_ref, target_ref, out_ref, held, rows, wide, table, ready, places, sems):
    load_labels = pltpu.make_async_copy(labels_ref, held, sems.at[0])
    load_labels.start()
    load_rows = pltpu.make_async_copy(rows_ref, rows, sems.at[1])
    load_rows.start()
    table[...] = jnp.full(table.shape, EMPTY, jnp.float32)
    load_labels.wait()
    blocks = held.shape[0]
    half = blocks // 2
    copies = [
        pltpu.make_async_copy(
            target_ref.at[pl.ds(k * half, half)], places.at[pl.ds(k * half, half)], sems.at[2 + k]
        )
        for k in range(2)
    ]

    def emit(b, line):
        target_ref[b : b + 1, :] = line
        if (b + 1) % half == 0:
            copies[b // half].start()

    slots_of(held[...], emit)
    load_rows.wait()
    wide[...] = rows[...].astype(jnp.float32)

    def block(b, carry):
        for j in range(128):
            table[pl.ds(places[b, j], 1), :] = wide[pl.ds(b * 128 + j, 1), :]
        return carry

    for k in range(2):
        copies[k].wait()
        lax.fori_loop(k * half, (k + 1) * half, block, 0)
    piece = table.shape[0] // PIECES
    stores = []
    for k in range(PIECES):
        part = pl.ds(k * piece, piece)
        ready[part, :] = table[part, :].astype(jnp.bfloat16)
        stores.append(pltpu.make_async_copy(ready.at[part], out_ref.at[part], sems.at[4 + k]))
        stores[-1].start()
    for store in stores:
        store.wait()


def dispatch(embedding, labels, slots):
    total = embedding.shape[0]
    return pl.pallas_call(
        dispatch_kernel,
        out_shape=(
            jax.ShapeDtypeStruct(labels.shape, jnp.int32),
            jax.ShapeDtypeStruct((slots, D), jnp.bfloat16),
        ),
        in_specs=[pl.BlockSpec(memory_space=pltpu.HBM)] * 2,
        out_specs=[
            pl.BlockSpec(memory_space=pltpu.VMEM),
            pl.BlockSpec(memory_space=pltpu.HBM),
        ],
        scratch_shapes=[
            pltpu.VMEM(labels.shape, jnp.int32),
            pltpu.VMEM((total, D), jnp.bfloat16),
            pltpu.VMEM((total, D), jnp.float32),
            pltpu.VMEM((slots, D), jnp.float32),
            pltpu.VMEM((slots, D), jnp.bfloat16),
            pltpu.SMEM(labels.shape, jnp.int32),
            pltpu.SemaphoreType.DMA((4 + PIECES,)),
        ],
        compiler_params=pltpu.CompilerParams(vmem_limit_bytes=WIDE_LIMIT),
    )(labels, embedding)


def eliminate(work, count, panel):
    pivots = [[] for _ in range(count)]
    lanes = iota((panel, D), 1)
    down = iota((panel, D), 0)
    for p in range(D // panel):
        base = p * panel
        tiles = [work[m, base : base + panel, :] for m in range(count)]
        diag = [jnp.ones((panel, D), jnp.float32) for _ in range(count)]
        for i in range(0, panel, STEP):
            inside = (lanes >= base + i) & (lanes < base + i + STEP)
            unit = jnp.where(lanes - base == down, 1.0, 0.0)
            for m in range(count):
                tile = tiles[m]
                columns = [
                    jnp.broadcast_to(tile[:, base + i + t : base + i + t + 1], (panel, D))
                    for t in range(STEP)
                ]
                small = [
                    [columns[v][i + t : i + t + 1, :] for v in range(STEP)] for t in range(STEP)
                ]
                tile = jnp.where(inside, unit, tile)
                lines = [tile[i + t : i + t + 1, :] for t in range(STEP)]
                for t in range(STEP):
                    inverse = 1.0 / small[t][t]
                    diag[m] = jnp.where(down == i + t, small[t][t], diag[m])
                    for u in range(t + 1, STEP):
                        ratio = small[t][u] * inverse
                        for v in range(u, STEP):
                            small[u][v] = small[u][v] - ratio * small[t][v]
                        columns[u] = columns[u] - ratio * columns[t]
                        lines[u] = lines[u] - ratio * lines[t]
                    factor = jnp.where(down > i + t, columns[t] * inverse, 0.0)
                    tile = tile - factor * lines[t]
                tiles[m] = tile
        for m in range(count):
            pivots[m].append(diag[m])
            work[m, base : base + panel, :] = tiles[m]
            below = base + panel
            if below < D:
                e1, e2, e3 = split3(tiles[m])
                n1, n2, n3 = split3(tiles[m] * (1.0 / diag[m]))
                left = jnp.concatenate([n1, n1, n2, n2, n1, n3], axis=0)
                right = jnp.concatenate([e1, e2, e1, e2, e3, e1], axis=0)
                step = lax.dot_general(
                    left,
                    right,
                    (((0,), (0,)), ((), ())),
                    preferred_element_type=jnp.float32,
                )
                old = work[m, below:, :]
                wide_lanes = iota(old.shape, 1)
                within = (wide_lanes >= base) & (wide_lanes < below)
                work[m, below:, :] = jnp.where(within, 0.0, old) - step[below:, :]
    return pivots


def log_sum(pivot_tiles):
    total = jnp.zeros((1, D), jnp.float32)
    for tile in pivot_tiles:
        total = total + jnp.sum(jnp.log(tile), axis=0, keepdims=True)
    return total


def posterior_scatter(second, first, number):
    same = iota((D, D), 0) == iota((D, D), 1)
    over = jnp.broadcast_to(first, (D, D))
    return jnp.where(same, 1.0, 0.0) + second - jnp.transpose(over) * over / (1.0 + number)


def moments_kernel(rows_ref, xt_ref, second_ref, info_ref, pack_ref, turned_ref, sems):
    stores = []
    depth = rows_ref.shape[0] * 16
    moments = []
    for c in range(2):
        rows = rows_ref[:, 16 * c : 16 * c + 16, :]
        wide = rows.astype(jnp.float32)
        empty = wide > 8.0
        wide = jnp.where(empty, 0.0, wide)
        first_tile = jnp.sum(wide, axis=0)
        number_tile = jnp.sum(jnp.where(empty, 0.0, 1.0), axis=0)
        clean = wide.astype(jnp.bfloat16).reshape(depth, D)
        turned = jnp.transpose(clean)
        turned_ref[c] = turned
        stores.append(pltpu.make_async_copy(turned_ref.at[c], xt_ref.at[c], sems.at[c]))
        stores[c].start()
        zero_side = (iota((D, depth), 1) & 8) == 0
        none = jnp.zeros_like(turned)
        left = jnp.concatenate(
            [jnp.where(zero_side, turned, none), jnp.where(zero_side, none, turned)], axis=0
        )
        second = jnp.dot(left, clean, preferred_element_type=jnp.float32)
        first = [jnp.sum(first_tile[8 * k : 8 * k + 8], axis=0, keepdims=True) for k in range(2)]
        number = [jnp.sum(number_tile[8 * k : 8 * k + 8], axis=0, keepdims=True) for k in range(2)]
        for s in range(2):
            m = 2 * c + s
            moments.append((second[s * D : (s + 1) * D], first[s], number[s]))
            second_ref[m] = moments[m][0]
    info_ref[...] = jnp.concatenate(
        [moments[m][1] for m in range(4)] + [moments[m][2] for m in range(4)], axis=0
    )
    whole = [tuple(a + b for a, b in zip(moments[2 * c], moments[2 * c + 1])) for c in range(2)]
    lower = iota((D, D), 0) >= iota((D, D), 1)
    same = iota((D, D), 0) == iota((D, D), 1)
    packed = jnp.where(lower, whole[0][0], whole[1][0])
    diagonal = jnp.sum(jnp.where(same, whole[1][0], 0.0), axis=0, keepdims=True)
    ending = jnp.concatenate(
        [diagonal, whole[0][1], whole[1][1], whole[0][2], whole[1][2], jnp.zeros((3, D), jnp.float32)],
        axis=0,
    )
    for q in range(pack_ref.shape[0]):
        pack_ref[q, 0:D, :] = packed
        pack_ref[q, D : D + 8, :] = ending
    for store in stores:
        store.wait()


def find_moments(arrived, owners):
    depth = arrived.shape[0] * 16
    f32 = jnp.float32
    return pl.pallas_call(
        moments_kernel,
        out_shape=(
            jax.ShapeDtypeStruct((FAR, D, depth), jnp.bfloat16),
            jax.ShapeDtypeStruct((4, D, D), f32),
            jax.ShapeDtypeStruct((8, D), f32),
            jax.ShapeDtypeStruct((owners, D + 8, D), f32),
        ),
        in_specs=[pl.BlockSpec(memory_space=pltpu.VMEM)],
        out_specs=[pl.BlockSpec(memory_space=pltpu.HBM)]
        + [pl.BlockSpec(memory_space=pltpu.VMEM)] * 3,
        scratch_shapes=[
            pltpu.VMEM((2, D, depth), jnp.bfloat16),
            pltpu.SemaphoreType.DMA((2,)),
        ],
        compiler_params=pltpu.CompilerParams(vmem_limit_bytes=VMEM_LIMIT),
        cost_estimate=pl.CostEstimate(flops=10**9, bytes_accessed=4 * 10**6, transcendentals=0),
    )(arrived)


def judge_kernel(logit_ref, far_ref, second_ref, info_ref, odds_ref, dets_ref, work, lines, xt_ref, sem):
    load = pltpu.make_async_copy(far_ref.at[0:2], xt_ref, sem)
    load.start()
    clusters, _, depth = xt_ref.shape
    firsts = [info_ref[m : m + 1, :] for m in range(4)]
    numbers = [info_ref[m : m + 1, :] for m in range(4, 8)]
    for m in range(4):
        work[m] = posterior_scatter(second_ref[m], firsts[m], numbers[m])
    pivots = eliminate(work, 4, 32)
    logdets = [log_sum(tiles) for tiles in pivots]
    dets_ref[...] = jnp.concatenate(logdets + numbers, axis=0)
    lower = iota((D, D), 0) >= iota((D, D), 1)
    lanes = iota((depth // 128, 128), 1)
    width = min(512, depth)
    odds = []
    load.wait()
    for c in range(clusters):
        offsets, shifts, pieces = [], [], []
        for t in range(2):
            m = 2 * c + t
            spread = jnp.concatenate(pivots[m], axis=0)
            unit = jnp.where(lower, work[m], 0.0)
            whiten = jnp.sqrt(numbers[m] + 2.0) * (unit * lax.rsqrt(spread))
            center = firsts[m] / (1.0 + numbers[m])
            shifted = jnp.sum(whiten * center, axis=1, keepdims=True)
            shifts.append(jnp.broadcast_to(shifted, (D, width)))
            pieces.append(jnp.concatenate(split3(whiten), axis=1))
            offsets.append(0.5 * D * jnp.log(numbers[m] + 2.0) - 0.5 * logdets[m])
        maps = jnp.concatenate(pieces, axis=0)
        shift = jnp.concatenate(shifts, axis=0)
        base = logit_ref[c] + (offsets[1] - offsets[0])
        for w in range(depth // width):
            columns = xt_ref[c, :, w * width : (w + 1) * width]
            image = jnp.dot(
                maps, jnp.concatenate([columns] * 3, axis=0), preferred_element_type=jnp.float32
            )
            image = image - shift
            squares = image * image
            gap = jnp.sum(squares[:D] - squares[D:], axis=0, keepdims=True)
            for v in range(width // 128):
                row = w * (width // 128) + v
                lines[row : row + 1, :] = gap[:, v * 128 : (v + 1) * 128]
        odds.append(1.0 / (1.0 + jnp.exp(-(base + 0.5 * lines[...]))))
    for s in range(8):
        first = pltpu.roll(odds[0], (128 - 16 * s) % 128, 1)
        second = pltpu.roll(odds[1], (144 - 16 * s) % 128, 1)
        odds_ref[pl.ds(s, depth // 128, stride=8), :] = jnp.where(lanes < 16, first, second)


def judge(logits, xt, second, info):
    depth = xt.shape[2]
    f32 = jnp.float32
    return pl.pallas_call(
        judge_kernel,
        out_shape=(
            jax.ShapeDtypeStruct((depth // 16, 128), f32),
            jax.ShapeDtypeStruct((8, D), f32),
        ),
        in_specs=[
            pl.BlockSpec(memory_space=pltpu.SMEM),
            pl.BlockSpec(memory_space=pltpu.HBM),
            pl.BlockSpec(memory_space=pltpu.VMEM),
            pl.BlockSpec(memory_space=pltpu.VMEM),
        ],
        out_specs=[pl.BlockSpec(memory_space=pltpu.VMEM)] * 2,
        scratch_shapes=[
            pltpu.VMEM((4, D, D), f32),
            pltpu.VMEM((depth // 128, 128), f32),
            pltpu.VMEM((2, D, depth), jnp.bfloat16),
            pltpu.SemaphoreType.DMA,
        ],
        compiler_params=pltpu.CompilerParams(vmem_limit_bytes=VMEM_LIMIT),
        cost_estimate=pl.CostEstimate(flops=10**10, bytes_accessed=10**7, transcendentals=0),
    )(logits, xt, second, info)


def unpack(pack):
    body = pack[0:D]
    flipped = jnp.transpose(body)
    low = iota((D, D), 0) > iota((D, D), 1)
    same = iota((D, D), 0) == iota((D, D), 1)
    second0 = jnp.where(low, body, flipped)
    second1 = jnp.where(same, pack[D : D + 1], jnp.where(low, flipped, body))
    return (
        (second0, pack[D + 1 : D + 2], pack[D + 3 : D + 4]),
        (second1, pack[D + 2 : D + 3], pack[D + 4 : D + 5]),
    )


def log_gamma(x):
    z = x + 8.0
    inverse = 1.0 / z
    square = inverse * inverse
    series = inverse * (1.0 / 12.0 - square * (1.0 / 360.0 - square * (1.0 / 1260.0)))
    low = x * (x + 1.0) * (x + 2.0) * (x + 3.0)
    high = (x + 4.0) * (x + 5.0) * (x + 6.0) * (x + 7.0)
    half_log_tau = 0.5 * math.log(2.0 * math.pi)
    return (z - 0.5) * jnp.log(z) - z + half_log_tau + series - jnp.log(low) - jnp.log(high)


def evidence(numbers, logdets):
    prior = D + 3.0
    half_steps = 0.5 * iota(numbers.shape, 1).astype(jnp.float32)
    terms = log_gamma(0.5 * (prior + numbers) - half_steps) - log_gamma(0.5 * prior - half_steps)
    return (
        -0.5 * D * math.log(math.pi) * numbers
        + jnp.sum(terms, axis=1, keepdims=True)
        - 0.5 * (prior + numbers) * logdets
        - 0.5 * D * jnp.log(1.0 + numbers)
        + log_gamma(numbers)
    )


def merge_kernel(mate_ref, dets_ref, own_ref, mate0_ref, mate1_ref, split_ref, join_ref, work):
    own = unpack(own_ref[...])
    mates = (unpack(mate0_ref[...])[0], unpack(mate1_ref[...])[1])
    both = tuple(tuple(a + b for a, b in zip(own[c], mates[c])) for c in range(2))
    stats = own + mates + both
    for m in range(6):
        work[m] = posterior_scatter(*stats[m])
    pivots = eliminate(work, 6, 16)
    blank = [jnp.ones((6, D), jnp.float32)]
    numbers = jnp.concatenate([dets_ref[4:8, :]] + [stats[m][2] for m in range(6)] + blank, axis=0)
    logdets = jnp.concatenate([dets_ref[0:4, :]] + [log_sum(pivots[m]) for m in range(6)] + blank, axis=0)
    value = evidence(numbers, logdets)
    for c in range(2):
        whole = value[4 + c : 5 + c]
        split = value[2 * c : 2 * c + 1] + value[2 * c + 1 : 2 * c + 2] - whole
        join = value[8 + c : 9 + c] - whole - value[6 + c : 7 + c]
        split_ref[c] = split[0, 0] * (1.0 / (D * D))
        join_ref[c] = join[0, 0] * (1.0 / (D * D))


def merge(mate, dets, own, everyone):
    block = (None,) + own.shape[1:]
    one = jax.ShapeDtypeStruct((2,), jnp.float32)
    return pl.pallas_call(
        merge_kernel,
        out_shape=(one, one),
        grid_spec=pltpu.PrefetchScalarGridSpec(
            num_scalar_prefetch=1,
            grid=(1,),
            in_specs=[
                pl.BlockSpec(dets.shape, lambda g, mate: (0, 0)),
                pl.BlockSpec(block, lambda g, mate: (0, 0, 0)),
                pl.BlockSpec(block, lambda g, mate: (mate[0], 0, 0)),
                pl.BlockSpec(block, lambda g, mate: (mate[1], 0, 0)),
            ],
            out_specs=[pl.BlockSpec(memory_space=pltpu.SMEM)] * 2,
            scratch_shapes=[pltpu.VMEM((6, D, D), jnp.float32)],
        ),
        compiler_params=pltpu.CompilerParams(vmem_limit_bytes=NARROW_LIMIT),
        cost_estimate=pl.CostEstimate(flops=MERGE_FLOPS, bytes_accessed=1, transcendentals=0),
    )(mate, dets, own, everyone, everyone)


def read_kernel(table_ref, target_ref, out_ref, lines):
    depth = table_ref.shape[0] // 4
    lanes = iota((depth, 128), 1)
    total = table_ref[pl.ds(0, depth, stride=4), 0, :]
    for q in range(1, 4):
        moved = pltpu.roll(table_ref[pl.ds(q, depth, stride=4), 0, :], 32 * q, 1)
        total = jnp.where(lanes >= 32 * q, moved, total)
    lines[...] = total
    target = target_ref[...]
    upper = target >> 7
    low = target & 127
    for g in range(target.shape[0] // 8):
        part = slice(8 * g, 8 * g + 8)
        total = jnp.zeros((8, 128), jnp.float32)
        for k in range(depth):
            line = jnp.broadcast_to(lines[k : k + 1, :], (8, 128))
            found = jnp.take_along_axis(line, low[part], axis=1)
            total = jnp.where(upper[part] == k, found, total)
        out_ref[part, :] = total


def read_back(table, target):
    return pl.pallas_call(
        read_kernel,
        out_shape=jax.ShapeDtypeStruct(target.shape, jnp.float32),
        scratch_shapes=[pltpu.VMEM((table.shape[0] // 4, 128), jnp.float32)],
        compiler_params=pltpu.CompilerParams(vmem_limit_bytes=NARROW_LIMIT),
    )(table, target)


def shards(embedding, assignment, sub_logit, merge_offset):
    owners, holders = lax.axis_size("own"), lax.axis_size("rows")
    experts = 2 * owners * sub_logit.shape[0]
    axes = ("own", "rows")
    devices = owners * holders
    labels = assignment.reshape(-1, 128)
    target, outgoing = dispatch(embedding, labels, experts * CAP)
    per_holder = merge_offset.shape[0]
    chunk = 2 * per_holder * CAP
    arrived = lax.all_to_all(
        outgoing.reshape(devices, chunk, D), axes, split_axis=0, concat_axis=0, tiled=True
    )
    logits = lax.dynamic_slice(sub_logit, (lax.axis_index("rows") * per_holder,), (per_holder,))
    xt, second, info, packs = find_moments(arrived, owners)
    everyone = lax.all_to_all(packs, "own", split_axis=0, concat_axis=0, tiled=True)
    odds, dets = judge(logits, xt, second, info)
    odds, everyone = lax.optimization_barrier((odds, everyone))
    returned = lax.all_to_all(
        odds.reshape(devices, 1, 128), axes, split_axis=0, concat_axis=0, tiled=True
    )
    mate = (lax.axis_index("own") + merge_offset) % owners
    split, join = merge(mate, dets, packs, everyone)
    sub_prob = read_back(returned, target).reshape(-1)
    return (sub_prob, split, join)


def solution(mesh):
    in_specs = (P(("rows", "own"), None), P(("rows", "own"), None), P("own"), P(("own", "rows")))
    out_specs = (P(("rows", "own")), P(("own", "rows")), P(("own", "rows")))
    return jax.shard_map(shards, mesh=mesh, in_specs=in_specs, out_specs=out_specs, check_vma=False)
```

```python
import math

import jax
import jax.numpy as jnp
from jax import lax
from jax.experimental import pallas as pl
from jax.experimental.pallas import tpu as pltpu
from jax.sharding import PartitionSpec as P

D = 128
CAP = 8
EMPTY = 64.0
VMEM_LIMIT = 48 * 1024 * 1024
WIDE_LIMIT = 60 * 1024 * 1024
MERGE_FLOPS = 1
FAR = 4
NARROW_LIMIT = 16 * 1024 * 1024
STEP = 4
PIECES = 4


def iota(shape, dim):
    return lax.broadcasted_iota(jnp.int32, shape, dim)


def split3(value):
    high = value.astype(jnp.bfloat16)
    rest = value - high.astype(jnp.float32)
    middle = rest.astype(jnp.bfloat16)
    low = (rest - middle.astype(jnp.float32)).astype(jnp.bfloat16)
    return high, middle, low


def slots_of(labels, emit):
    blocks = labels.shape[0]
    flipped = jnp.transpose(labels.astype(jnp.float32))
    before = iota((128, 128), 0) < iota((128, 128), 1)
    lanes = iota((128, 128), 1)
    levels = iota((8, 128), 0)
    running = jnp.zeros((8, 128), jnp.float32)
    for b in range(blocks):
        across = labels[b : b + 1, :]
        down = jnp.broadcast_to(flipped[:, b : b + 1], (128, 128)).astype(jnp.int32)
        same = jnp.where((down == across) & before, 1.0, 0.0)
        inside = jnp.sum(same, axis=0, keepdims=True)
        low = across & 127
        upper = levels == (across >> 7)
        found = jnp.take_along_axis(running, jnp.broadcast_to(low, (8, 128)), axis=1)
        earlier = jnp.sum(jnp.where(upper, found, 0.0), axis=0, keepdims=True)
        emit(b, across * CAP + (inside + earlier).astype(jnp.int32))
        hot_low = jnp.where((down & 127) == lanes, 1.0, 0.0).astype(jnp.bfloat16)
        hot_up = jnp.where(upper, 1.0, 0.0).astype(jnp.bfloat16)
        running = running + jnp.dot(hot_up, hot_low, preferred_element_type=jnp.float32)


def dispatch_kernel(labels_ref, rows_ref, target_ref, out_ref, held, rows, wide, table, ready, places, sems):
    load_labels = pltpu.make_async_copy(labels_ref, held, sems.at[0])
    load_labels.start()
    load_rows = pltpu.make_async_copy(rows_ref, rows, sems.at[1])
    load_rows.start()
    table[...] = jnp.full(table.shape, EMPTY, jnp.float32)
    load_labels.wait()
    blocks = held.shape[0]
    half = blocks // 2
    copies = [
        pltpu.make_async_copy(
            target_ref.at[pl.ds(k * half, half)], places.at[pl.ds(k * half, half)], sems.at[2 + k]
        )
        for k in range(2)
    ]

    def emit(b, line):
        target_ref[b : b + 1, :] = line
        if (b + 1) % half == 0:
            copies[b // half].start()

    slots_of(held[...], emit)
    load_rows.wait()
    wide[...] = rows[...].astype(jnp.float32)

    def block(b, carry):
        for j in range(128):
            table[pl.ds(places[b, j], 1), :] = wide[pl.ds(b * 128 + j, 1), :]
        return carry

    for k in range(2):
        copies[k].wait()
        lax.fori_loop(k * half, (k + 1) * half, block, 0)
    piece = table.shape[0] // PIECES
    stores = []
    for k in range(PIECES):
        part = pl.ds(k * piece, piece)
        ready[part, :] = table[part, :].astype(jnp.bfloat16)
        stores.append(pltpu.make_async_copy(ready.at[part], out_ref.at[part], sems.at[4 + k]))
        stores[-1].start()
    for store in stores:
        store.wait()


def dispatch(embedding, labels, slots):
    total = embedding.shape[0]
    return pl.pallas_call(
        dispatch_kernel,
        out_shape=(
            jax.ShapeDtypeStruct(labels.shape, jnp.int32),
            jax.ShapeDtypeStruct((slots, D), jnp.bfloat16),
        ),
        in_specs=[pl.BlockSpec(memory_space=pltpu.HBM)] * 2,
        out_specs=[
            pl.BlockSpec(memory_space=pltpu.VMEM),
            pl.BlockSpec(memory_space=pltpu.HBM),
        ],
        scratch_shapes=[
            pltpu.VMEM(labels.shape, jnp.int32),
            pltpu.VMEM((total, D), jnp.bfloat16),
            pltpu.VMEM((total, D), jnp.float32),
            pltpu.VMEM((slots, D), jnp.float32),
            pltpu.VMEM((slots, D), jnp.bfloat16),
            pltpu.SMEM(labels.shape, jnp.int32),
            pltpu.SemaphoreType.DMA((4 + PIECES,)),
        ],
        compiler_params=pltpu.CompilerParams(vmem_limit_bytes=WIDE_LIMIT),
    )(labels, embedding)


def eliminate(work, count, panel):
    pivots = [[] for _ in range(count)]
    lanes = iota((panel, D), 1)
    down = iota((panel, D), 0)
    for p in range(D // panel):
        base = p * panel
        tiles = [work[m, base : base + panel, :] for m in range(count)]
        diag = [jnp.ones((panel, D), jnp.float32) for _ in range(count)]
        for i in range(0, panel, STEP):
            inside = (lanes >= base + i) & (lanes < base + i + STEP)
            unit = jnp.where(lanes - base == down, 1.0, 0.0)
            for m in range(count):
                tile = tiles[m]
                columns = [
                    jnp.broadcast_to(tile[:, base + i + t : base + i + t + 1], (panel, D))
                    for t in range(STEP)
                ]
                small = [
                    [columns[v][i + t : i + t + 1, :] for v in range(STEP)] for t in range(STEP)
                ]
                tile = jnp.where(inside, unit, tile)
                lines = [tile[i + t : i + t + 1, :] for t in range(STEP)]
                for t in range(STEP):
                    inverse = 1.0 / small[t][t]
                    diag[m] = jnp.where(down == i + t, small[t][t], diag[m])
                    for u in range(t + 1, STEP):
                        ratio = small[t][u] * inverse
                        for v in range(u, STEP):
                            small[u][v] = small[u][v] - ratio * small[t][v]
                        columns[u] = columns[u] - ratio * columns[t]
                        lines[u] = lines[u] - ratio * lines[t]
                    factor = jnp.where(down > i + t, columns[t] * inverse, 0.0)
                    tile = tile - factor * lines[t]
                tiles[m] = tile
        for m in range(count):
            pivots[m].append(diag[m])
            work[m, base : base + panel, :] = tiles[m]
            below = base + panel
            if below < D:
                e1, e2, e3 = split3(tiles[m])
                n1, n2, n3 = split3(tiles[m] * (1.0 / diag[m]))
                left = jnp.concatenate([n1, n1, n2, n2, n1, n3], axis=0)
                right = jnp.concatenate([e1, e2, e1, e2, e3, e1], axis=0)
                step = lax.dot_general(
                    left,
                    right,
                    (((0,), (0,)), ((), ())),
                    preferred_element_type=jnp.float32,
                )
                old = work[m, below:, :]
                wide_lanes = iota(old.shape, 1)
                within = (wide_lanes >= base) & (wide_lanes < below)
                work[m, below:, :] = jnp.where(within, 0.0, old) - step[below:, :]
    return pivots


def log_sum(pivot_tiles):
    total = jnp.zeros((1, D), jnp.float32)
    for tile in pivot_tiles:
        total = total + jnp.sum(jnp.log(tile), axis=0, keepdims=True)
    return total


def posterior_scatter(second, first, number):
    same = iota((D, D), 0) == iota((D, D), 1)
    column = jnp.transpose(jnp.broadcast_to(first, (8, D)))[:, 0:1]
    return jnp.where(same, 1.0, 0.0) + second - column * first / (1.0 + number)


def moments_kernel(rows_ref, far_ref, second_ref, info_ref, pack_ref, sem):
    sources = rows_ref.shape[0]
    keep = pltpu.make_async_copy(rows_ref, far_ref.at[pl.ds(0, sources)], sem)
    keep.start()
    depth = sources * 16
    moments = []
    for c in range(2):
        rows = rows_ref[:, 16 * c : 16 * c + 16, :]
        wide = rows.astype(jnp.float32)
        empty = wide > 8.0
        wide = jnp.where(empty, 0.0, wide)
        first_tile = jnp.sum(wide, axis=0)
        number_tile = jnp.sum(jnp.where(empty, 0.0, 1.0), axis=0)
        clean = wide.astype(jnp.bfloat16).reshape(depth, D)
        turned = jnp.transpose(clean)
        zero_side = (iota((D, depth), 1) & 8) == 0
        none = jnp.zeros_like(turned)
        left = jnp.concatenate(
            [jnp.where(zero_side, turned, none), jnp.where(zero_side, none, turned)], axis=0
        )
        second = jnp.dot(left, clean, preferred_element_type=jnp.float32)
        first = [jnp.sum(first_tile[8 * k : 8 * k + 8], axis=0, keepdims=True) for k in range(2)]
        number = [jnp.sum(number_tile[8 * k : 8 * k + 8], axis=0, keepdims=True) for k in range(2)]
        for s in range(2):
            m = 2 * c + s
            moments.append((second[s * D : (s + 1) * D], first[s], number[s]))
            second_ref[m] = moments[m][0]
    info_ref[...] = jnp.concatenate(
        [moments[m][1] for m in range(4)] + [moments[m][2] for m in range(4)], axis=0
    )
    whole = [tuple(a + b for a, b in zip(moments[2 * c], moments[2 * c + 1])) for c in range(2)]
    lower = iota((D, D), 0) >= iota((D, D), 1)
    same = iota((D, D), 0) == iota((D, D), 1)
    packed = jnp.where(lower, whole[0][0], whole[1][0])
    diagonal = jnp.sum(jnp.where(same, whole[1][0], 0.0), axis=0, keepdims=True)
    ending = jnp.concatenate(
        [diagonal, whole[0][1], whole[1][1], whole[0][2], whole[1][2], jnp.zeros((3, D), jnp.float32)],
        axis=0,
    )
    for q in range(pack_ref.shape[0]):
        pack_ref[q, 0:D, :] = packed
        pack_ref[q, D : D + 8, :] = ending
    keep.wait()


def find_moments(arrived, owners):
    sources, chunk, _ = arrived.shape
    f32 = jnp.float32
    return pl.pallas_call(
        moments_kernel,
        out_shape=(
            jax.ShapeDtypeStruct((FAR * sources, chunk, D), jnp.bfloat16),
            jax.ShapeDtypeStruct((4, D, D), f32),
            jax.ShapeDtypeStruct((8, D), f32),
            jax.ShapeDtypeStruct((owners, D + 8, D), f32),
        ),
        in_specs=[pl.BlockSpec(memory_space=pltpu.VMEM)],
        out_specs=[pl.BlockSpec(memory_space=pltpu.HBM)]
        + [pl.BlockSpec(memory_space=pltpu.VMEM)] * 3,
        scratch_shapes=[pltpu.SemaphoreType.DMA],
        compiler_params=pltpu.CompilerParams(vmem_limit_bytes=VMEM_LIMIT),
        cost_estimate=pl.CostEstimate(flops=10**9, bytes_accessed=4 * 10**6, transcendentals=0),
    )(arrived)


def judge_kernel(logit_ref, far_ref, second_ref, info_ref, odds_ref, dets_ref, work, lines, rows_ref, sem):
    sources = rows_ref.shape[0]
    load = pltpu.make_async_copy(far_ref.at[pl.ds(0, sources)], rows_ref, sem)
    load.start()
    clusters, depth = 2, sources * 16
    firsts = [info_ref[m : m + 1, :] for m in range(4)]
    numbers = [info_ref[m : m + 1, :] for m in range(4, 8)]
    for m in range(4):
        work[m] = posterior_scatter(second_ref[m], firsts[m], numbers[m])
    pivots = eliminate(work, 4, 32)
    logdets = [log_sum(tiles) for tiles in pivots]
    dets_ref[...] = jnp.concatenate(logdets + numbers, axis=0)
    lower = iota((D, D), 0) >= iota((D, D), 1)
    lanes = iota((depth // 128, 128), 1)
    width = min(512, depth)
    odds = []
    load.wait()
    for c in range(clusters):
        offsets, shifts, pieces = [], [], []
        for t in range(2):
            m = 2 * c + t
            spread = jnp.concatenate(pivots[m], axis=0)
            unit = jnp.where(lower, work[m], 0.0)
            whiten = jnp.sqrt(numbers[m] + 2.0) * (unit * lax.rsqrt(spread))
            center = firsts[m] / (1.0 + numbers[m])
            shifted = jnp.sum(whiten * center, axis=1, keepdims=True)
            shifts.append(jnp.broadcast_to(shifted, (D, width)))
            pieces.append(jnp.concatenate(split3(whiten), axis=1))
            offsets.append(0.5 * D * jnp.log(numbers[m] + 2.0) - 0.5 * logdets[m])
        maps = jnp.concatenate(pieces, axis=0)
        shift = jnp.concatenate(shifts, axis=0)
        base = logit_ref[c] + (offsets[1] - offsets[0])
        for w in range(depth // width):
            part = slice(w * (width // 16), (w + 1) * (width // 16))
            rows = rows_ref[part, 16 * c : 16 * c + 16, :].reshape(width, D)
            image = lax.dot_general(
                maps,
                jnp.concatenate([rows] * 3, axis=1),
                (((1,), (1,)), ((), ())),
                preferred_element_type=jnp.float32,
            )
            image = image - shift
            squares = image * image
            gap = jnp.sum(squares[:D] - squares[D:], axis=0, keepdims=True)
            for v in range(width // 128):
                row = w * (width // 128) + v
                lines[row : row + 1, :] = gap[:, v * 128 : (v + 1) * 128]
        odds.append(1.0 / (1.0 + jnp.exp(-(base + 0.5 * lines[...]))))
    for s in range(8):
        first = pltpu.roll(odds[0], (128 - 16 * s) % 128, 1)
        second = pltpu.roll(odds[1], (144 - 16 * s) % 128, 1)
        odds_ref[pl.ds(s, depth // 128, stride=8), :] = jnp.where(lanes < 16, first, second)


def judge(logits, far, second, info):
    sources, chunk = far.shape[0] // FAR, far.shape[1]
    f32 = jnp.float32
    return pl.pallas_call(
        judge_kernel,
        out_shape=(
            jax.ShapeDtypeStruct((sources, 128), f32),
            jax.ShapeDtypeStruct((8, D), f32),
        ),
        in_specs=[
            pl.BlockSpec(memory_space=pltpu.SMEM),
            pl.BlockSpec(memory_space=pltpu.HBM),
            pl.BlockSpec(memory_space=pltpu.VMEM),
            pl.BlockSpec(memory_space=pltpu.VMEM),
        ],
        out_specs=[pl.BlockSpec(memory_space=pltpu.VMEM)] * 2,
        scratch_shapes=[
            pltpu.VMEM((4, D, D), f32),
            pltpu.VMEM((sources // 8, 128), f32),
            pltpu.VMEM((sources, chunk, D), jnp.bfloat16),
            pltpu.SemaphoreType.DMA,
        ],
        compiler_params=pltpu.CompilerParams(vmem_limit_bytes=VMEM_LIMIT),
        cost_estimate=pl.CostEstimate(flops=10**10, bytes_accessed=10**7, transcendentals=0),
    )(logits, far, second, info)


def unpack(pack):
    body = pack[0:D]
    flipped = jnp.transpose(body)
    low = iota((D, D), 0) > iota((D, D), 1)
    same = iota((D, D), 0) == iota((D, D), 1)
    second0 = jnp.where(low, body, flipped)
    second1 = jnp.where(same, pack[D : D + 1], jnp.where(low, flipped, body))
    return (
        (second0, pack[D + 1 : D + 2], pack[D + 3 : D + 4]),
        (second1, pack[D + 2 : D + 3], pack[D + 4 : D + 5]),
    )


def log_gamma(x):
    z = x + 8.0
    inverse = 1.0 / z
    square = inverse * inverse
    series = inverse * (1.0 / 12.0 - square * (1.0 / 360.0 - square * (1.0 / 1260.0)))
    low = x * (x + 1.0) * (x + 2.0) * (x + 3.0)
    high = (x + 4.0) * (x + 5.0) * (x + 6.0) * (x + 7.0)
    half_log_tau = 0.5 * math.log(2.0 * math.pi)
    return (z - 0.5) * jnp.log(z) - z + half_log_tau + series - jnp.log(low) - jnp.log(high)


def evidence(numbers, logdets):
    prior = D + 3.0
    half_steps = 0.5 * iota(numbers.shape, 1).astype(jnp.float32)
    terms = log_gamma(0.5 * (prior + numbers) - half_steps) - log_gamma(0.5 * prior - half_steps)
    return (
        -0.5 * D * math.log(math.pi) * numbers
        + jnp.sum(terms, axis=1, keepdims=True)
        - 0.5 * (prior + numbers) * logdets
        - 0.5 * D * jnp.log(1.0 + numbers)
        + log_gamma(numbers)
    )


def merge_kernel(mate_ref, dets_ref, own_ref, mate0_ref, mate1_ref, split_ref, join_ref, work):
    own = unpack(own_ref[...])
    mates = (unpack(mate0_ref[...])[0], unpack(mate1_ref[...])[1])
    both = tuple(tuple(a + b for a, b in zip(own[c], mates[c])) for c in range(2))
    stats = own + mates + both
    for m in range(6):
        work[m] = posterior_scatter(*stats[m])
    pivots = eliminate(work, 6, 16)
    blank = [jnp.ones((6, D), jnp.float32)]
    numbers = jnp.concatenate([dets_ref[4:8, :]] + [stats[m][2] for m in range(6)] + blank, axis=0)
    logdets = jnp.concatenate([dets_ref[0:4, :]] + [log_sum(pivots[m]) for m in range(6)] + blank, axis=0)
    value = evidence(numbers, logdets)
    for c in range(2):
        whole = value[4 + c : 5 + c]
        split = value[2 * c : 2 * c + 1] + value[2 * c + 1 : 2 * c + 2] - whole
        join = value[8 + c : 9 + c] - whole - value[6 + c : 7 + c]
        split_ref[c] = split[0, 0] * (1.0 / (D * D))
        join_ref[c] = join[0, 0] * (1.0 / (D * D))


def merge(mate, dets, own, everyone):
    block = (None,) + own.shape[1:]
    one = jax.ShapeDtypeStruct((2,), jnp.float32)
    return pl.pallas_call(
        merge_kernel,
        out_shape=(one, one),
        grid_spec=pltpu.PrefetchScalarGridSpec(
            num_scalar_prefetch=1,
            grid=(1,),
            in_specs=[
                pl.BlockSpec(dets.shape, lambda g, mate: (0, 0)),
                pl.BlockSpec(block, lambda g, mate: (0, 0, 0)),
                pl.BlockSpec(block, lambda g, mate: (mate[0], 0, 0)),
                pl.BlockSpec(block, lambda g, mate: (mate[1], 0, 0)),
            ],
            out_specs=[pl.BlockSpec(memory_space=pltpu.SMEM)] * 2,
            scratch_shapes=[pltpu.VMEM((6, D, D), jnp.float32)],
        ),
        compiler_params=pltpu.CompilerParams(vmem_limit_bytes=NARROW_LIMIT),
        cost_estimate=pl.CostEstimate(flops=MERGE_FLOPS, bytes_accessed=1, transcendentals=0),
    )(mate, dets, own, everyone, everyone)


def read_kernel(table_ref, target_ref, out_ref, lines):
    depth = table_ref.shape[0] // 4
    lanes = iota((depth, 128), 1)
    total = table_ref[pl.ds(0, depth, stride=4), 0, :]
    for q in range(1, 4):
        moved = pltpu.roll(table_ref[pl.ds(q, depth, stride=4), 0, :], 32 * q, 1)
        total = jnp.where(lanes >= 32 * q, moved, total)
    lines[...] = total
    target = target_ref[...]
    upper = target >> 7
    low = target & 127
    for g in range(target.shape[0] // 8):
        part = slice(8 * g, 8 * g + 8)
        total = jnp.zeros((8, 128), jnp.float32)
        for k in range(depth):
            line = jnp.broadcast_to(lines[k : k + 1, :], (8, 128))
            found = jnp.take_along_axis(line, low[part], axis=1)
            total = jnp.where(upper[part] == k, found, total)
        out_ref[part, :] = total


def read_back(table, target):
    return pl.pallas_call(
        read_kernel,
        out_shape=jax.ShapeDtypeStruct(target.shape, jnp.float32),
        scratch_shapes=[pltpu.VMEM((table.shape[0] // 4, 128), jnp.float32)],
        compiler_params=pltpu.CompilerParams(vmem_limit_bytes=NARROW_LIMIT),
    )(table, target)


def shards(embedding, assignment, sub_logit, merge_offset):
    owners, holders = lax.axis_size("own"), lax.axis_size("rows")
    experts = 2 * owners * sub_logit.shape[0]
    axes = ("own", "rows")
    devices = owners * holders
    labels = assignment.reshape(-1, 128)
    target, outgoing = dispatch(embedding, labels, experts * CAP)
    per_holder = merge_offset.shape[0]
    chunk = 2 * per_holder * CAP
    arrived = lax.all_to_all(
        outgoing.reshape(devices, chunk, D), axes, split_axis=0, concat_axis=0, tiled=True
    )
    logits = lax.dynamic_slice(sub_logit, (lax.axis_index("rows") * per_holder,), (per_holder,))
    far, second, info, packs = find_moments(arrived, owners)
    everyone = lax.all_to_all(packs, "own", split_axis=0, concat_axis=0, tiled=True)
    odds, dets = judge(logits, far, second, info)
    odds, everyone = lax.optimization_barrier((odds, everyone))
    returned = lax.all_to_all(
        odds.reshape(devices, 1, 128), axes, split_axis=0, concat_axis=0, tiled=True
    )
    mate = (lax.axis_index("own") + merge_offset) % owners
    split, join = merge(mate, dets, packs, everyone)
    sub_prob = read_back(returned, target).reshape(-1)
    return (sub_prob, split, join)


def solution(mesh):
    in_specs = (P(("rows", "own"), None), P(("rows", "own"), None), P("own"), P(("own", "rows")))
    out_specs = (P(("rows", "own")), P(("own", "rows")), P(("own", "rows")))
    return jax.shard_map(shards, mesh=mesh, in_specs=in_specs, out_specs=out_specs, check_vma=False)
```

```python
import math

import jax
import jax.numpy as jnp
from jax import lax
from jax.experimental import pallas as pl
from jax.experimental.pallas import tpu as pltpu
from jax.sharding import PartitionSpec as P

D = 128
CAP = 8
EMPTY = 64.0
VMEM_LIMIT = 48 * 1024 * 1024
WIDE_LIMIT = 60 * 1024 * 1024
MERGE_FLOPS = 1
FAR = 4
NARROW_LIMIT = 16 * 1024 * 1024
STEP = 4
PIECES = 4


def iota(shape, dim):
    return lax.broadcasted_iota(jnp.int32, shape, dim)


def split3(value):
    high = value.astype(jnp.bfloat16)
    rest = value - high.astype(jnp.float32)
    middle = rest.astype(jnp.bfloat16)
    low = (rest - middle.astype(jnp.float32)).astype(jnp.bfloat16)
    return high, middle, low


def slots_of(labels, emit):
    blocks = labels.shape[0]
    flipped = jnp.transpose(labels.astype(jnp.float32))
    before = iota((128, 128), 0) < iota((128, 128), 1)
    lanes = iota((128, 128), 1)
    levels = iota((8, 128), 0)
    running = jnp.zeros((8, 128), jnp.float32)
    for b in range(blocks):
        across = labels[b : b + 1, :]
        down = jnp.broadcast_to(flipped[:, b : b + 1], (128, 128)).astype(jnp.int32)
        same = jnp.where((down == across) & before, 1.0, 0.0)
        inside = jnp.sum(same, axis=0, keepdims=True)
        low = across & 127
        upper = levels == (across >> 7)
        found = jnp.take_along_axis(running, jnp.broadcast_to(low, (8, 128)), axis=1)
        earlier = jnp.sum(jnp.where(upper, found, 0.0), axis=0, keepdims=True)
        emit(b, across * CAP + (inside + earlier).astype(jnp.int32))
        hot_low = jnp.where((down & 127) == lanes, 1.0, 0.0).astype(jnp.bfloat16)
        hot_up = jnp.where(upper, 1.0, 0.0).astype(jnp.bfloat16)
        running = running + jnp.dot(hot_up, hot_low, preferred_element_type=jnp.float32)


def dispatch_kernel(labels_ref, rows_ref, target_ref, out_ref, held, rows, wide, table, ready, places, sems):
    load_labels = pltpu.make_async_copy(labels_ref, held, sems.at[0])
    load_labels.start()
    load_rows = pltpu.make_async_copy(rows_ref, rows, sems.at[1])
    load_rows.start()
    table[...] = jnp.full(table.shape, EMPTY, jnp.float32)
    load_labels.wait()
    blocks = held.shape[0]
    half = blocks // 2
    copies = [
        pltpu.make_async_copy(
            target_ref.at[pl.ds(k * half, half)], places.at[pl.ds(k * half, half)], sems.at[2 + k]
        )
        for k in range(2)
    ]

    load_rows.wait()
    wide[...] = rows[...].astype(jnp.float32)

    def block(b, carry):
        for j in range(128):
            table[pl.ds(places[b, j], 1), :] = wide[pl.ds(b * 128 + j, 1), :]
        return carry

    def emit(b, line):
        target_ref[b : b + 1, :] = line
        if (b + 1) % half == 0:
            copies[b // half].start()
        if b == half:
            copies[0].wait()
        if b >= half:
            block(b - half, 0)

    slots_of(held[...], emit)
    copies[1].wait()
    lax.fori_loop(half, blocks, block, 0)
    piece = table.shape[0] // PIECES
    stores = []
    for k in range(PIECES):
        part = pl.ds(k * piece, piece)
        ready[part, :] = table[part, :].astype(jnp.bfloat16)
        stores.append(pltpu.make_async_copy(ready.at[part], out_ref.at[part], sems.at[4 + k]))
        stores[-1].start()
    for store in stores:
        store.wait()


def dispatch(embedding, labels, slots):
    total = embedding.shape[0]
    return pl.pallas_call(
        dispatch_kernel,
        out_shape=(
            jax.ShapeDtypeStruct(labels.shape, jnp.int32),
            jax.ShapeDtypeStruct((slots, D), jnp.bfloat16),
        ),
        in_specs=[pl.BlockSpec(memory_space=pltpu.HBM)] * 2,
        out_specs=[
            pl.BlockSpec(memory_space=pltpu.VMEM),
            pl.BlockSpec(memory_space=pltpu.HBM),
        ],
        scratch_shapes=[
            pltpu.VMEM(labels.shape, jnp.int32),
            pltpu.VMEM((total, D), jnp.bfloat16),
            pltpu.VMEM((total, D), jnp.float32),
            pltpu.VMEM((slots, D), jnp.float32),
            pltpu.VMEM((slots, D), jnp.bfloat16),
            pltpu.SMEM(labels.shape, jnp.int32),
            pltpu.SemaphoreType.DMA((4 + PIECES,)),
        ],
        compiler_params=pltpu.CompilerParams(vmem_limit_bytes=WIDE_LIMIT),
    )(labels, embedding)


def eliminate(work, count, panel):
    pivots = [[] for _ in range(count)]
    lanes = iota((panel, D), 1)
    down = iota((panel, D), 0)
    for p in range(D // panel):
        base = p * panel
        tiles = [work[m, base : base + panel, :] for m in range(count)]
        diag = [jnp.ones((panel, D), jnp.float32) for _ in range(count)]
        for i in range(0, panel, STEP):
            inside = (lanes >= base + i) & (lanes < base + i + STEP)
            unit = jnp.where(lanes - base == down, 1.0, 0.0)
            for m in range(count):
                tile = tiles[m]
                columns = [
                    jnp.broadcast_to(tile[:, base + i + t : base + i + t + 1], (panel, D))
                    for t in range(STEP)
                ]
                small = [
                    [columns[v][i + t : i + t + 1, :] for v in range(STEP)] for t in range(STEP)
                ]
                tile = jnp.where(inside, unit, tile)
                lines = [tile[i + t : i + t + 1, :] for t in range(STEP)]
                for t in range(STEP):
                    inverse = 1.0 / small[t][t]
                    diag[m] = jnp.where(down == i + t, small[t][t], diag[m])
                    for u in range(t + 1, STEP):
                        ratio = small[t][u] * inverse
                        for v in range(u, STEP):
                            small[u][v] = small[u][v] - ratio * small[t][v]
                        columns[u] = columns[u] - ratio * columns[t]
                        lines[u] = lines[u] - ratio * lines[t]
                    factor = jnp.where(down > i + t, columns[t] * inverse, 0.0)
                    tile = tile - factor * lines[t]
                tiles[m] = tile
        for m in range(count):
            pivots[m].append(diag[m])
            work[m, base : base + panel, :] = tiles[m]
            below = base + panel
            if below < D:
                e1, e2, e3 = split3(tiles[m])
                n1, n2, n3 = split3(tiles[m] * (1.0 / diag[m]))
                left = jnp.concatenate([n1, n1, n2, n2, n1, n3], axis=0)
                right = jnp.concatenate([e1, e2, e1, e2, e3, e1], axis=0)
                step = lax.dot_general(
                    left,
                    right,
                    (((0,), (0,)), ((), ())),
                    preferred_element_type=jnp.float32,
                )
                old = work[m, below:, :]
                wide_lanes = iota(old.shape, 1)
                within = (wide_lanes >= base) & (wide_lanes < below)
                work[m, below:, :] = jnp.where(within, 0.0, old) - step[below:, :]
    return pivots


def log_sum(pivot_tiles):
    total = jnp.zeros((1, D), jnp.float32)
    for tile in pivot_tiles:
        total = total + jnp.sum(jnp.log(tile), axis=0, keepdims=True)
    return total


def posterior_scatter(second, first, number):
    same = iota((D, D), 0) == iota((D, D), 1)
    column = jnp.transpose(jnp.broadcast_to(first, (8, D)))[:, 0:1]
    return jnp.where(same, 1.0, 0.0) + second - column * first / (1.0 + number)


def moments_kernel(rows_ref, far_ref, second_ref, info_ref, pack_ref, sem):
    sources = rows_ref.shape[0]
    keep = pltpu.make_async_copy(rows_ref, far_ref.at[pl.ds(0, sources)], sem)
    keep.start()
    depth = sources * 16
    moments = []
    for c in range(2):
        rows = rows_ref[:, 16 * c : 16 * c + 16, :]
        wide = rows.astype(jnp.float32)
        empty = wide > 8.0
        wide = jnp.where(empty, 0.0, wide)
        first_tile = jnp.sum(wide, axis=0)
        number_tile = jnp.sum(jnp.where(empty, 0.0, 1.0), axis=0)
        clean = wide.astype(jnp.bfloat16).reshape(depth, D)
        turned = jnp.transpose(clean)
        zero_side = (iota((D, depth), 1) & 8) == 0
        none = jnp.zeros_like(turned)
        left = jnp.concatenate(
            [jnp.where(zero_side, turned, none), jnp.where(zero_side, none, turned)], axis=0
        )
        second = jnp.dot(left, clean, preferred_element_type=jnp.float32)
        first = [jnp.sum(first_tile[8 * k : 8 * k + 8], axis=0, keepdims=True) for k in range(2)]
        number = [jnp.sum(number_tile[8 * k : 8 * k + 8], axis=0, keepdims=True) for k in range(2)]
        for s in range(2):
            m = 2 * c + s
            moments.append((second[s * D : (s + 1) * D], first[s], number[s]))
            second_ref[m] = moments[m][0]
    info_ref[...] = jnp.concatenate(
        [moments[m][1] for m in range(4)] + [moments[m][2] for m in range(4)], axis=0
    )
    whole = [tuple(a + b for a, b in zip(moments[2 * c], moments[2 * c + 1])) for c in range(2)]
    lower = iota((D, D), 0) >= iota((D, D), 1)
    same = iota((D, D), 0) == iota((D, D), 1)
    packed = jnp.where(lower, whole[0][0], whole[1][0])
    diagonal = jnp.sum(jnp.where(same, whole[1][0], 0.0), axis=0, keepdims=True)
    ending = jnp.concatenate(
        [diagonal, whole[0][1], whole[1][1], whole[0][2], whole[1][2], jnp.zeros((3, D), jnp.float32)],
        axis=0,
    )
    for q in range(pack_ref.shape[0]):
        pack_ref[q, 0:D, :] = packed
        pack_ref[q, D : D + 8, :] = ending
    keep.wait()


def find_moments(arrived, owners):
    sources, chunk, _ = arrived.shape
    f32 = jnp.float32
    return pl.pallas_call(
        moments_kernel,
        out_shape=(
            jax.ShapeDtypeStruct((FAR * sources, chunk, D), jnp.bfloat16),
            jax.ShapeDtypeStruct((4, D, D), f32),
            jax.ShapeDtypeStruct((8, D), f32),
            jax.ShapeDtypeStruct((owners, D + 8, D), f32),
        ),
        in_specs=[pl.BlockSpec(memory_space=pltpu.VMEM)],
        out_specs=[pl.BlockSpec(memory_space=pltpu.HBM)]
        + [pl.BlockSpec(memory_space=pltpu.VMEM)] * 3,
        scratch_shapes=[pltpu.SemaphoreType.DMA],
        compiler_params=pltpu.CompilerParams(vmem_limit_bytes=VMEM_LIMIT),
        cost_estimate=pl.CostEstimate(flops=10**9, bytes_accessed=4 * 10**6, transcendentals=0),
    )(arrived)


def judge_kernel(logit_ref, far_ref, second_ref, info_ref, odds_ref, dets_ref, work, lines, rows_ref, sem):
    sources = rows_ref.shape[0]
    load = pltpu.make_async_copy(far_ref.at[pl.ds(0, sources)], rows_ref, sem)
    load.start()
    clusters, depth = 2, sources * 16
    firsts = [info_ref[m : m + 1, :] for m in range(4)]
    numbers = [info_ref[m : m + 1, :] for m in range(4, 8)]
    for m in range(4):
        work[m] = posterior_scatter(second_ref[m], firsts[m], numbers[m])
    pivots = eliminate(work, 4, 32)
    logdets = [log_sum(tiles) for tiles in pivots]
    dets_ref[...] = jnp.concatenate(logdets + numbers, axis=0)
    lower = iota((D, D), 0) >= iota((D, D), 1)
    lanes = iota((depth // 128, 128), 1)
    width = min(512, depth)
    odds = []
    load.wait()
    for c in range(clusters):
        offsets, shifts, pieces = [], [], []
        for t in range(2):
            m = 2 * c + t
            spread = jnp.concatenate(pivots[m], axis=0)
            unit = jnp.where(lower, work[m], 0.0)
            whiten = jnp.sqrt(numbers[m] + 2.0) * (unit * lax.rsqrt(spread))
            center = firsts[m] / (1.0 + numbers[m])
            shifted = jnp.sum(whiten * center, axis=1, keepdims=True)
            shifts.append(jnp.broadcast_to(shifted, (D, width)))
            pieces.append(jnp.concatenate(split3(whiten), axis=1))
            offsets.append(0.5 * D * jnp.log(numbers[m] + 2.0) - 0.5 * logdets[m])
        maps = jnp.concatenate(pieces, axis=0)
        shift = jnp.concatenate(shifts, axis=0)
        base = logit_ref[c] + (offsets[1] - offsets[0])
        for w in range(depth // width):
            part = slice(w * (width // 16), (w + 1) * (width // 16))
            rows = rows_ref[part, 16 * c : 16 * c + 16, :].reshape(width, D)
            image = lax.dot_general(
                maps,
                jnp.concatenate([rows] * 3, axis=1),
                (((1,), (1,)), ((), ())),
                preferred_element_type=jnp.float32,
            )
            image = image - shift
            squares = image * image
            gap = jnp.sum(squares[:D] - squares[D:], axis=0, keepdims=True)
            for v in range(width // 128):
                row = w * (width // 128) + v
                lines[row : row + 1, :] = gap[:, v * 128 : (v + 1) * 128]
        odds.append(1.0 / (1.0 + jnp.exp(-(base + 0.5 * lines[...]))))
    for s in range(8):
        first = pltpu.roll(odds[0], (128 - 16 * s) % 128, 1)
        second = pltpu.roll(odds[1], (144 - 16 * s) % 128, 1)
        odds_ref[pl.ds(s, depth // 128, stride=8), :] = jnp.where(lanes < 16, first, second)


def judge(logits, far, second, info):
    sources, chunk = far.shape[0] // FAR, far.shape[1]
    f32 = jnp.float32
    return pl.pallas_call(
        judge_kernel,
        out_shape=(
            jax.ShapeDtypeStruct((sources, 128), f32),
            jax.ShapeDtypeStruct((8, D), f32),
        ),
        in_specs=[
            pl.BlockSpec(memory_space=pltpu.SMEM),
            pl.BlockSpec(memory_space=pltpu.HBM),
            pl.BlockSpec(memory_space=pltpu.VMEM),
            pl.BlockSpec(memory_space=pltpu.VMEM),
        ],
        out_specs=[pl.BlockSpec(memory_space=pltpu.VMEM)] * 2,
        scratch_shapes=[
            pltpu.VMEM((4, D, D), f32),
            pltpu.VMEM((sources // 8, 128), f32),
            pltpu.VMEM((sources, chunk, D), jnp.bfloat16),
            pltpu.SemaphoreType.DMA,
        ],
        compiler_params=pltpu.CompilerParams(vmem_limit_bytes=VMEM_LIMIT),
        cost_estimate=pl.CostEstimate(flops=10**10, bytes_accessed=10**7, transcendentals=0),
    )(logits, far, second, info)


def unpack(pack):
    body = pack[0:D]
    flipped = jnp.transpose(body)
    low = iota((D, D), 0) > iota((D, D), 1)
    same = iota((D, D), 0) == iota((D, D), 1)
    second0 = jnp.where(low, body, flipped)
    second1 = jnp.where(same, pack[D : D + 1], jnp.where(low, flipped, body))
    return (
        (second0, pack[D + 1 : D + 2], pack[D + 3 : D + 4]),
        (second1, pack[D + 2 : D + 3], pack[D + 4 : D + 5]),
    )


def log_gamma(x):
    z = x + 8.0
    inverse = 1.0 / z
    square = inverse * inverse
    series = inverse * (1.0 / 12.0 - square * (1.0 / 360.0 - square * (1.0 / 1260.0)))
    low = x * (x + 1.0) * (x + 2.0) * (x + 3.0)
    high = (x + 4.0) * (x + 5.0) * (x + 6.0) * (x + 7.0)
    half_log_tau = 0.5 * math.log(2.0 * math.pi)
    return (z - 0.5) * jnp.log(z) - z + half_log_tau + series - jnp.log(low) - jnp.log(high)


def evidence(numbers, logdets):
    prior = D + 3.0
    half_steps = 0.5 * iota(numbers.shape, 1).astype(jnp.float32)
    terms = log_gamma(0.5 * (prior + numbers) - half_steps) - log_gamma(0.5 * prior - half_steps)
    return (
        -0.5 * D * math.log(math.pi) * numbers
        + jnp.sum(terms, axis=1, keepdims=True)
        - 0.5 * (prior + numbers) * logdets
        - 0.5 * D * jnp.log(1.0 + numbers)
        + log_gamma(numbers)
    )


def merge_kernel(mate_ref, dets_ref, own_ref, mate0_ref, mate1_ref, split_ref, join_ref, work):
    own = unpack(own_ref[...])
    mates = (unpack(mate0_ref[...])[0], unpack(mate1_ref[...])[1])
    both = tuple(tuple(a + b for a, b in zip(own[c], mates[c])) for c in range(2))
    stats = own + mates + both
    for m in range(6):
        work[m] = posterior_scatter(*stats[m])
    pivots = eliminate(work, 6, 16)
    blank = [jnp.ones((6, D), jnp.float32)]
    numbers = jnp.concatenate([dets_ref[4:8, :]] + [stats[m][2] for m in range(6)] + blank, axis=0)
    logdets = jnp.concatenate([dets_ref[0:4, :]] + [log_sum(pivots[m]) for m in range(6)] + blank, axis=0)
    value = evidence(numbers, logdets)
    for c in range(2):
        whole = value[4 + c : 5 + c]
        split = value[2 * c : 2 * c + 1] + value[2 * c + 1 : 2 * c + 2] - whole
        join = value[8 + c : 9 + c] - whole - value[6 + c : 7 + c]
        split_ref[c] = split[0, 0] * (1.0 / (D * D))
        join_ref[c] = join[0, 0] * (1.0 / (D * D))


def merge(mate, dets, own, everyone):
    block = (None,) + own.shape[1:]
    one = jax.ShapeDtypeStruct((2,), jnp.float32)
    return pl.pallas_call(
        merge_kernel,
        out_shape=(one, one),
        grid_spec=pltpu.PrefetchScalarGridSpec(
            num_scalar_prefetch=1,
            grid=(1,),
            in_specs=[
                pl.BlockSpec(dets.shape, lambda g, mate: (0, 0)),
                pl.BlockSpec(block, lambda g, mate: (0, 0, 0)),
                pl.BlockSpec(block, lambda g, mate: (mate[0], 0, 0)),
                pl.BlockSpec(block, lambda g, mate: (mate[1], 0, 0)),
            ],
            out_specs=[pl.BlockSpec(memory_space=pltpu.SMEM)] * 2,
            scratch_shapes=[pltpu.VMEM((6, D, D), jnp.float32)],
        ),
        compiler_params=pltpu.CompilerParams(vmem_limit_bytes=NARROW_LIMIT),
        cost_estimate=pl.CostEstimate(flops=MERGE_FLOPS, bytes_accessed=1, transcendentals=0),
    )(mate, dets, own, everyone, everyone)


def read_kernel(table_ref, target_ref, out_ref, lines):
    depth = table_ref.shape[0] // 4
    lanes = iota((depth, 128), 1)
    total = table_ref[pl.ds(0, depth, stride=4), 0, :]
    for q in range(1, 4):
        moved = pltpu.roll(table_ref[pl.ds(q, depth, stride=4), 0, :], 32 * q, 1)
        total = jnp.where(lanes >= 32 * q, moved, total)
    lines[...] = total
    target = target_ref[...]
    upper = target >> 7
    low = target & 127
    for g in range(target.shape[0] // 8):
        part = slice(8 * g, 8 * g + 8)
        total = jnp.zeros((8, 128), jnp.float32)
        for k in range(depth):
            line = jnp.broadcast_to(lines[k : k + 1, :], (8, 128))
            found = jnp.take_along_axis(line, low[part], axis=1)
            total = jnp.where(upper[part] == k, found, total)
        out_ref[part, :] = total


def read_back(table, target):
    return pl.pallas_call(
        read_kernel,
        out_shape=jax.ShapeDtypeStruct(target.shape, jnp.float32),
        scratch_shapes=[pltpu.VMEM((table.shape[0] // 4, 128), jnp.float32)],
        compiler_params=pltpu.CompilerParams(vmem_limit_bytes=NARROW_LIMIT),
    )(table, target)


def shards(embedding, assignment, sub_logit, merge_offset):
    owners, holders = lax.axis_size("own"), lax.axis_size("rows")
    experts = 2 * owners * sub_logit.shape[0]
    axes = ("own", "rows")
    devices = owners * holders
    labels = assignment.reshape(-1, 128)
    target, outgoing = dispatch(embedding, labels, experts * CAP)
    per_holder = merge_offset.shape[0]
    chunk = 2 * per_holder * CAP
    arrived = lax.all_to_all(
        outgoing.reshape(devices, chunk, D), axes, split_axis=0, concat_axis=0, tiled=True
    )
    logits = lax.dynamic_slice(sub_logit, (lax.axis_index("rows") * per_holder,), (per_holder,))
    far, second, info, packs = find_moments(arrived, owners)
    everyone = lax.all_to_all(packs, "own", split_axis=0, concat_axis=0, tiled=True)
    odds, dets = judge(logits, far, second, info)
    odds, everyone = lax.optimization_barrier((odds, everyone))
    returned = lax.all_to_all(
        odds.reshape(devices, 1, 128), axes, split_axis=0, concat_axis=0, tiled=True
    )
    mate = (lax.axis_index("own") + merge_offset) % owners
    split, join = merge(mate, dets, packs, everyone)
    sub_prob = read_back(returned, target).reshape(-1)
    return (sub_prob, split, join)


def solution(mesh):
    in_specs = (P(("rows", "own"), None), P(("rows", "own"), None), P("own"), P(("own", "rows")))
    out_specs = (P(("rows", "own")), P(("own", "rows")), P(("own", "rows")))
    return jax.shard_map(shards, mesh=mesh, in_specs=in_specs, out_specs=out_specs, check_vma=False)
```
